32 devices in a mesh: dev: 32 (over z, y, x, core).
Axes of the slice: x: 2, y: 2, z: 4, core: 2. Of those that a mesh axis runs over, the one named last changes fastest.
Arguments:
- images: bfloat16 [384, 14, 14, 512], P('dev'), may hold values from -6 to 6
- cotangent: bfloat16 [384, 14, 14, 512], P('dev'), may hold values from -6 to 6
- image_counts: int32 [32], P('dev'), may hold values from 6 to 12, as said below
- rel_index: int32 [49, 49], replicated, may hold values from 0 to 168, as said below
- ln1_gain: bfloat16 [512], P('dev'), may hold values from 0.5 to 1.5
- ln1_shift: bfloat16 [512], P('dev'), may hold values from -1.75 to 1.75
- w_qkv: bfloat16 [512, 1536], P('dev'), may hold values from -0.25 to 0.25
- q_bias: bfloat16 [512], P('dev'), may hold values from -3 to 3
- v_bias: bfloat16 [512], P('dev'), may hold values from -3 to 3
- w_proj: bfloat16 [512, 512], P('dev'), may hold values from -0.75 to 0.75
- b_proj: bfloat16 [512], P('dev'), may hold values from -1.75 to 1.75
- ln2_gain: bfloat16 [512], P('dev'), may hold values from 0.5 to 1.5
- ln2_shift: bfloat16 [512], P('dev'), may hold values from -1.75 to 1.75
- w_fc1: bfloat16 [512, 2048], P('dev'), may hold values from -0.25 to 0.25
- b_fc1: bfloat16 [2048], P('dev'), may hold values from -3 to 3
- w_fc2: bfloat16 [2048, 512], P('dev'), may hold values from -0.1875 to 0.1875
- b_fc2: bfloat16 [512], P('dev'), may hold values from -1.75 to 1.75
- bias_table: float32 [169, 16], replicated, may hold values from -5 to 5
Outputs:
- output: bfloat16 [384, 14, 14, 512], P('dev')
- grad_images: bfloat16 [384, 14, 14, 512], P('dev')
- grad_ln1_gain: float32 [512], P('dev')
- grad_ln1_shift: float32 [512], P('dev')
- grad_w_qkv: float32 [512, 1536], P('dev')
- grad_q_bias: float32 [512], P('dev')
- grad_v_bias: float32 [512], P('dev')
- grad_w_proj: float32 [512, 512], P('dev')
- grad_b_proj: float32 [512], P('dev')
- grad_ln2_gain: float32 [512], P('dev')
- grad_ln2_shift: float32 [512], P('dev')
- grad_w_fc1: float32 [512, 2048], P('dev')
- grad_b_fc1: float32 [2048], P('dev')
- grad_w_fc2: float32 [2048, 512], P('dev')
- grad_b_fc2: float32 [512], P('dev')
- grad_bias_table: float32 [169, 16], replicated
The draws below stay inside these ranges and needn't reach their ends.
Inputs may be any that keep to these rules, and one draw needn't show every extreme that they name: `image_counts`: each device holds at least half of its 12 slots live; in every draw some device is full. `rel_index`: entry (i, j) names the table row of the offset between token i and token j of a window; equal offsets share a row, unequal offsets have different rows.
All inputs are finite; a program needn't handle non-finite values.
Results may differ from the reference program's by a relative error of at most 0.012.
Values may be sent and summed in bfloat16 or wider, within the bound.
No kernel may reach another device: no remote copies, remote signals or barrier semaphores. Data moves between devices by JAX's collectives and lax.ppermute only.
A program may use at most 256 MiB of HBM per device.

```python
import jax
import jax.numpy as jnp
from jax import lax

D = 512
FF = 2048
HEADS = 16
WINDOW = 7
SIDE = 14
TABLE = 169
SLOTS = 12
IMAGES = 384


def draw_image_counts(key, part):
    key = jax.random.fold_in(key, 11)
    count_key, full_key, least_key = jax.random.split(key, 3)
    groups = IMAGES // SLOTS
    counts = jax.random.randint(count_key, (groups,), (SLOTS + 1) // 2, SLOTS + 1)
    full_place = jax.random.randint(full_key, (), 0, groups)
    least_place = (full_place + 1 + jax.random.randint(least_key, (), 0, groups - 1)) % groups
    places = jnp.arange(groups)
    counts = jnp.where(places == full_place, SLOTS, counts)
    counts = jnp.where(places == least_place, (SLOTS + 1) // 2, counts)
    return counts.astype(jnp.int32)


def draw_rel_index(key, part):
    key = jax.random.fold_in(key, 23)
    span = 2 * WINDOW - 1
    order = jax.random.permutation(key, span * span)
    places = jnp.arange(WINDOW * WINDOW)
    row_of = places // WINDOW
    col_of = places % WINDOW
    offset = (row_of[:, None] - row_of[None, :] + WINDOW - 1) * span + (col_of[:, None] - col_of[None, :] + WINDOW - 1)
    return order[offset].astype(jnp.int32)


def levels(stream_key, shape, shards, low, top_value):
    def one(axis_at, blocks):
        draws = jax.random.uniform(jax.random.fold_in(jax.random.fold_in(stream_key, 6), axis_at), (blocks,), jnp.float32, low / len(shards), top_value / len(shards))
        return jnp.repeat(jnp.exp(draws), shape[axis_at] // blocks).reshape((-1,) + (1,) * (len(shape) - axis_at - 1))

    loudness = one(*shards[0])
    for cut in shards[1:]:
        loudness = loudness * one(*cut)
    return loudness


def bell_draw(rng, shape, scale, most, cuts=(), held_as=jnp.bfloat16):
    values = jax.random.normal(rng, shape, jnp.float32) * scale
    if len(cuts) > 0:
        values = levels(rng, shape, cuts, -0.22, 0.18) * values
    return jnp.clip(values, min=-most, max=most).astype(held_as)


def setup_inputs(seed: int = 0) -> dict:
    splits = jax.random.split(jax.random.key(seed), 19)
    images = bell_draw(splits[0], (IMAGES, SIDE, SIDE, D), 1.0, 6.0, ((0, 32),))
    cotangent = bell_draw(splits[1], (IMAGES, SIDE, SIDE, D), 1.0, 6.0, ((0, 32),))
    image_counts = draw_image_counts(jax.random.fold_in(splits[18], 71), 0)
    rel_index = draw_rel_index(jax.random.fold_in(splits[18], 71), 0)
    ln1_gain = jnp.clip(1.0 + 0.1 * jax.random.normal(splits[4], (D,), jnp.float32), 0.5, 1.5).astype(jnp.bfloat16)
    ln1_shift = bell_draw(splits[5], (D,), 0.3, 1.75, ((0, 32),))
    w_qkv = bell_draw(splits[6], (D, 3 * D), D ** -0.5, 0.25, ((0, 32),))
    q_bias = bell_draw(splits[7], (D,), 0.5, 3.0, ((0, 32),))
    v_bias = bell_draw(splits[8], (D,), 0.5, 3.0, ((0, 32),))
    w_proj = bell_draw(splits[9], (D, D), (D // 8) ** -0.5, 0.75, ((0, 32),))
    b_proj = bell_draw(splits[10], (D,), 0.3, 1.75, ((0, 32),))
    ln2_gain = jnp.clip(1.0 + 0.1 * jax.random.normal(splits[11], (D,), jnp.float32), 0.5, 1.5).astype(jnp.bfloat16)
    ln2_shift = bell_draw(splits[12], (D,), 0.3, 1.75, ((0, 32),))
    w_fc1 = bell_draw(splits[13], (D, FF), D ** -0.5, 0.25, ((0, 32),))
    b_fc1 = bell_draw(splits[14], (FF,), 0.5, 3.0, ((0, 32),))
    w_fc2 = bell_draw(splits[15], (FF, D), (FF // 2) ** -0.5, 0.1875, ((0, 32),))
    b_fc2 = bell_draw(splits[16], (D,), 0.3, 1.75, ((0, 32),))
    bias_table = bell_draw(splits[17], (TABLE, HEADS), 1.0, 5.0, (), jnp.float32)
    return {"images": images, "cotangent": cotangent, "image_counts": image_counts, "rel_index": rel_index, "ln1_gain": ln1_gain, "ln1_shift": ln1_shift, "w_qkv": w_qkv, "q_bias": q_bias, "v_bias": v_bias, "w_proj": w_proj, "b_proj": b_proj, "ln2_gain": ln2_gain, "ln2_shift": ln2_shift, "w_fc1": w_fc1, "b_fc1": b_fc1, "w_fc2": w_fc2, "b_fc2": b_fc2, "bias_table": bias_table}


EPSILON = 1e-05
HIGHEST = lax.Precision.HIGHEST

@jax.custom_vjp
def low(v):
    return lax.optimization_barrier(v.astype(jnp.bfloat16)).astype(jnp.float32)

@jax.custom_vjp
def low_back(v):
    return v

def low_keep(v):
    return (low(v), None)

def low_pass(kept, grad):
    return (grad,)

def back_keep(v):
    return (v, None)

def back_low(kept, grad):
    return (low(grad),)
low.defvjp(low_keep, low_pass)
low_back.defvjp(back_keep, back_low)

def layer_norm(values, gain, shift):
    center = values - lax.optimization_barrier(jnp.mean(values, -1, keepdims=True))
    spread = lax.optimization_barrier(jnp.mean(center * center, -1, keepdims=True))
    return center * lax.rsqrt(spread + EPSILON) * gain + shift

def to_windows(images):
    slots = images.shape[0]
    width = images.shape[3]
    split = images.reshape(slots, SIDE // WINDOW, WINDOW, SIDE // WINDOW, WINDOW, width)
    return split.transpose(0, 1, 3, 2, 4, 5).reshape(-1, width)

def from_windows(rows, slots):
    width = rows.shape[1]
    split = rows.reshape(slots, SIDE // WINDOW, SIDE // WINDOW, WINDOW, WINDOW, width)
    return split.transpose(0, 1, 3, 2, 4, 5).reshape(slots, SIDE, SIDE, width)

def block_forward(params, inputs, alive_rows, rel_index):
    gain_one, shift_one, qkv_weight, query_bias, value_bias, proj_weight, proj_bias, gain_two, shift_two, fc1_weight, fc1_bias, fc2_weight, fc2_bias, table = params
    area = WINDOW * WINDOW
    rows = inputs.shape[0]
    windows = rows // area
    normed_one = low(layer_norm(inputs, gain_one, shift_one))
    qkv_bias = jnp.concatenate([query_bias, jnp.zeros_like(query_bias), value_bias])
    triple = low(low_back(jnp.dot(normed_one, qkv_weight, precision=HIGHEST) + qkv_bias))
    view = triple.reshape(windows, area, 3, HEADS, D // HEADS)
    queries = view[:, :, 0]
    keys = view[:, :, 1]
    values = view[:, :, 2]
    rel_bias = table[rel_index.reshape(-1)].reshape(area, area, HEADS).transpose(2, 0, 1)
    scale = (D // HEADS) ** (-0.5)
    scores = jnp.einsum('wqhd,wkhd->whqk', queries, keys, precision=HIGHEST) * scale + rel_bias
    scores = low_back(scores)
    probs = low(jax.nn.softmax(scores, -1))
    mixed = jnp.einsum('whqk,wkhd->wqhd', probs, values, precision=HIGHEST).reshape(rows, D)
    mixed = low(low_back(mixed))
    branch = low_back(jnp.dot(mixed, proj_weight, precision=HIGHEST) + proj_bias)
    residual = inputs + branch
    normed_two = low(layer_norm(residual, gain_two, shift_two))
    hidden = low_back(jnp.dot(normed_two, fc1_weight, precision=HIGHEST) + fc1_bias)
    activated = low(jax.nn.gelu(hidden, approximate=False))
    second = low_back(jnp.dot(activated, fc2_weight, precision=HIGHEST) + fc2_bias)
    return (residual + second) * alive_rows

def reference(images, cotangent, image_counts, rel_index, ln1_gain, ln1_shift, w_qkv, q_bias, v_bias, w_proj, b_proj, ln2_gain, ln2_shift, w_fc1, b_fc1, w_fc2, b_fc2, bias_table):
    params = tuple((item.astype(jnp.float32) for item in (ln1_gain, ln1_shift, w_qkv, q_bias, v_bias, w_proj, b_proj, ln2_gain, ln2_shift, w_fc1, b_fc1, w_fc2, b_fc2, bias_table)))
    groups = image_counts.shape[0]
    grouped_images = images.reshape(groups, SLOTS, SIDE, SIDE, D)
    grouped_cot = cotangent.reshape(groups, SLOTS, SIDE, SIDE, D)

    def one_group(totals, items):
        group_images, group_cot, count = items
        inputs = to_windows(group_images).astype(jnp.float32)
        alive = (jnp.arange(SLOTS, dtype=jnp.int32) < count).astype(jnp.float32)
        alive_rows = jnp.repeat(alive, SIDE * SIDE)[:, None]

        def forward(prm, values):
            return block_forward(prm, values, alive_rows, rel_index)
        result, pullback = jax.vjp(forward, params, inputs)
        grads, grad_in = pullback(to_windows(group_cot).astype(jnp.float32))
        totals = jax.tree.map(lambda left, right: left + right, totals, grads)
        outs = (from_windows(result, SLOTS).astype(jnp.bfloat16), from_windows(grad_in, SLOTS).astype(jnp.bfloat16))
        return (totals, outs)
    zeros = jax.tree.map(jnp.zeros_like, params)
    totals, (outputs, grad_all) = lax.scan(one_group, zeros, (grouped_images, grouped_cot, image_counts))
    g_gain_one, g_shift_one, g_qkv, g_qbias, g_vbias, g_proj, g_pbias, g_gain_two, g_shift_two, g_fc1, g_fbias_one, g_fc2, g_fbias_two, g_table = totals
    return (outputs.reshape(images.shape), grad_all.reshape(images.shape), g_gain_one, g_shift_one, g_qkv, g_qbias, g_vbias, g_proj, g_pbias, g_gain_two, g_shift_two, g_fc1, g_fbias_one, g_fc2, g_fbias_two, g_table)
```

```python
from functools import partial

import jax
import jax.numpy as jnp
import numpy as np
from jax import lax
from jax.experimental import pallas as pl
from jax.experimental.pallas import tpu as pltpu
from jax.sharding import PartitionSpec as P

WINDOW = 7
SIDE = 14
COLS = 16
PAIR = WINDOW * COLS
KEYS = 128
LANES = 128
EPSILON = 1e-05
HIGHEST = lax.Precision.HIGHEST
MIB = 2**20
NEG = -1e30
F32 = jnp.float32
BF16 = jnp.bfloat16


def dot(left, right):
    return lax.dot_general(left, right, (((1,), (0,)), ((), ())), preferred_element_type=F32)


def dot_nt(left, right):
    return lax.dot_general(left, right, (((1,), (1,)), ((), ())), preferred_element_type=F32)


def dot_tn(left, right):
    return lax.dot_general(left, right, (((0,), (0,)), ((), ())), preferred_element_type=F32)


def padded_rows(block):
    wide = block.astype(F32)
    wide = jnp.pad(wide, ((0, 0), (0, 0), (0, COLS - SIDE), (0, 0)))
    return wide.reshape(-1, block.shape[-1])


def unpadded(rows, images):
    return rows.reshape(images, SIDE, COLS, rows.shape[-1])[:, :, :SIDE, :]


def moments(values):
    center = values - jnp.mean(values, -1, keepdims=True)
    spread = jnp.mean(center * center, -1, keepdims=True)
    scale = lax.rsqrt(spread + EPSILON)
    return center * scale, scale


def norm_backward(grad, hat, scale, gain):
    inner = grad * gain
    mean_one = jnp.mean(inner, -1, keepdims=True)
    mean_two = jnp.mean(inner * hat, -1, keepdims=True)
    return scale * (inner - mean_one - hat * mean_two)


def head_masks(head_dim):
    lane = lax.broadcasted_iota(jnp.int32, (1, LANES), 1) // head_dim
    return [lane == h for h in range(LANES // head_dim)]


def stacked(block, masks):
    zero = jnp.zeros_like(block)
    return jnp.concatenate([jnp.where(m, block, zero) for m in masks], 0)


def side_by_side(tall, parts):
    rows = tall.shape[0] // parts
    return jnp.concatenate([tall[i * rows : (i + 1) * rows] for i in range(parts)], 1)


def forward_kernel(heads, img_ref, w_ref, vec_ref, bias_ref, *refs):
    triple_ref, probs_ref, mixed_ref, trip = refs[-4:]
    group = img_ref.shape[0]
    width = img_ref.shape[-1]
    head_dim = width // heads
    scale = head_dim ** (-0.5)
    per = LANES // head_dim
    rows = group * SIDE * COLS
    inputs = padded_rows(img_ref[...])
    hat, _ = moments(inputs)
    normed = (hat * vec_ref[0:1, :width] + vec_ref[1:2, :width]).astype(BF16)
    triple = (dot(normed, w_ref[...]) + vec_ref[2:3, :]).astype(BF16)
    trip[0:rows, :] = triple
    trip[rows:, :] = jnp.zeros((COLS, 3 * width), BF16)
    triple_ref[...] = triple.reshape(group, SIDE * COLS, 3 * width)
    masks = head_masks(head_dim)

    def pair(p, carry):
        start = pl.multiple_of(p * PAIR, COLS)
        for g in range(width // LANES):
            q = trip[pl.ds(start, PAIR), g * LANES : (g + 1) * LANES]
            k = trip[pl.ds(start, KEYS), width + g * LANES : width + (g + 1) * LANES]
            v = trip[pl.ds(start, KEYS), 2 * width + g * LANES : 2 * width + (g + 1) * LANES]
            scores = dot_nt(stacked(q, masks), k) * scale + bias_ref[g]
            top = jnp.max(scores, -1, keepdims=True)
            raised = jnp.exp(scores - top)
            total = jnp.sum(raised, -1, keepdims=True)
            probs = (raised / total).astype(BF16)
            probs_ref[p, g] = probs
            mixed = dot(side_by_side(probs, per), stacked(v, masks))
            mixed_ref[p, :, g * LANES : (g + 1) * LANES] = mixed.astype(BF16)
        return carry

    lax.fori_loop(0, 2 * group, pair, 0)


def mlp_kernel(
    counts_ref, img_ref, cot_ref, mixed_ref, wp_ref, w1_ref, w2_ref, vec_ref, b1_ref,
    out_ref, gres_ref, gmix_ref, g1_ref, g2_ref, gp_ref, gvec_ref, gb1_ref,
    acc1, acc2, accp, accv, accb,
):
    step = pl.program_id(0)
    group = img_ref.shape[0]
    width = img_ref.shape[-1]
    rows = group * SIDE * COLS
    chunks = w1_ref.shape[0]

    @pl.when(step == 0)
    def _():
        for ref in (acc1, acc2, accp, accv, accb):
            ref[...] = jnp.zeros_like(ref)

    row = lax.broadcasted_iota(jnp.int32, (rows, 1), 0)
    image = row // (SIDE * COLS)
    live = ((step * group + image) < counts_ref[0]) & (row % COLS < SIDE)
    mixed = mixed_ref[...].reshape(rows, width)
    residual = padded_rows(img_ref[...]) + dot(mixed, wp_ref[...]) + vec_ref[0:1, :]
    hat, scale = moments(residual)
    gain = vec_ref[1:2, :]
    normed = (hat * gain + vec_ref[2:3, :]).astype(BF16)
    normed_t = normed.T
    grad_out = jnp.where(live, padded_rows(cot_ref[...]), 0.0)
    grad_low = grad_out.astype(BF16)
    grad_low_t = grad_low.T

    def chunk(c, carry):
        total, back = carry
        hidden = dot(normed, w1_ref[c]) + b1_ref[c]
        size = jnp.abs(hidden)
        bell = jnp.exp(-0.5 * hidden * hidden)
        t = 1.0 / (1.0 + (0.3275911 * 0.7071067811865476) * size)
        poly = t * (
            0.254829592
            + t * (-0.284496736 + t * (1.421413741 + t * (-1.453152027 + t * 1.061405429)))
        )
        tail = 0.5 * poly * bell
        below = jnp.where(hidden < 0, tail, 1.0 - tail)
        act = (hidden * below).astype(BF16)
        slope = below + hidden * (0.3989422804014327 * bell)
        total = total + dot(act, w2_ref[c])
        grad_hidden = (slope * dot_nt(grad_low, w2_ref[c])).astype(BF16)
        back = back + dot_nt(grad_hidden, w1_ref[c])
        acc1[c] += dot(normed_t, grad_hidden)
        acc2[c] += dot(grad_low_t, act)
        accb[c, 0:1] += jnp.sum(grad_hidden.astype(F32), 0, keepdims=True)
        return total, back

    zeros = jnp.zeros((rows, width), F32)
    total, back = lax.fori_loop(0, chunks, chunk, (zeros, zeros))
    result = jnp.where(live, residual + total + vec_ref[3:4, :], 0.0)
    out_ref[...] = unpadded(result, group).astype(BF16)
    grad_res = grad_out + norm_backward(back, hat, scale, gain)
    gres_ref[...] = grad_res.reshape(group, SIDE * COLS, width)
    grad_res_low = grad_res.astype(BF16)
    gmix_ref[...] = dot_nt(grad_res_low, wp_ref[...]).astype(BF16).reshape(group, SIDE * COLS, width)
    accp[...] += dot(mixed.T, grad_res_low)
    accv[0:1] += jnp.sum(grad_res_low.astype(F32), 0, keepdims=True)
    accv[1:2] += jnp.sum(back * hat, 0, keepdims=True)
    accv[2:3] += jnp.sum(back, 0, keepdims=True)
    accv[3:4] += jnp.sum(grad_low.astype(F32), 0, keepdims=True)

    @pl.when(step == pl.num_programs(0) - 1)
    def _():
        g1_ref[...] = acc1[...].astype(BF16)
        for c in range(chunks):
            g2_ref[c] = acc2[c].astype(BF16).T
        gp_ref[...] = accp[...].astype(BF16)
        gvec_ref[...] = accv[...]
        gb1_ref[...] = accb[...]


def backward_kernel(heads, img_ref, gres_ref, gmix_ref, triple_ref, probs_ref, w_ref, vec_ref, *refs):
    gin_ref, gw_ref, gvec_ref, gtrip_ref, gbias_ref, trip, gtrip, accw, accv, accb = refs[-10:]
    carried = refs[:-10]
    step = pl.program_id(0)
    group = img_ref.shape[0]
    width = img_ref.shape[-1]
    head_dim = width // heads
    scale = head_dim ** (-0.5)
    per = LANES // head_dim
    rows = group * SIDE * COLS

    @pl.when(step == 0)
    def _():
        if carried:
            accw[...] = carried[1][...]
            accv[...] = carried[2][...]
            accb[...] = carried[4][...]
            gtrip_ref[...] = carried[3][...]
        else:
            accw[...] = jnp.zeros_like(accw)
            accv[...] = jnp.zeros_like(accv)
            accb[...] = jnp.zeros_like(accb)
            gtrip_ref[...] = jnp.zeros_like(gtrip_ref)

    trip[0:rows, :] = triple_ref[...].reshape(rows, 3 * width)
    trip[rows:, :] = jnp.zeros((COLS, 3 * width), BF16)
    masks = head_masks(head_dim)

    def pair(p, carry):
        start = pl.multiple_of(p * PAIR, COLS)
        for g in range(width // LANES):
            lo, hi = g * LANES, (g + 1) * LANES
            q = trip[pl.ds(start, PAIR), lo:hi]
            k = trip[pl.ds(start, KEYS), width + lo : width + hi]
            v = trip[pl.ds(start, KEYS), 2 * width + lo : 2 * width + hi]
            probs = probs_ref[p, g]
            grad_mixed = stacked(gmix_ref[p, :, lo:hi], masks)
            wide = probs.astype(F32)
            grad_probs = dot_nt(grad_mixed, v)
            inner = jnp.sum(wide * grad_probs, -1, keepdims=True)
            grad_scores = (wide * (grad_probs - inner)).astype(BF16)
            accb[g] += grad_scores.astype(F32)
            grad_q = dot(side_by_side(grad_scores, per), stacked(k, masks)) * scale
            grad_k = dot_tn(grad_scores, stacked(q, masks)) * scale
            grad_v = dot_tn(probs, grad_mixed)
            gtrip[pl.ds(start, PAIR), lo:hi] = grad_q.astype(BF16)
            gtrip[pl.ds(start, PAIR), width + lo : width + hi] = grad_k[:PAIR].astype(BF16)
            gtrip[pl.ds(start, PAIR), 2 * width + lo : 2 * width + hi] = grad_v[:PAIR].astype(BF16)
        return carry

    lax.fori_loop(0, 2 * group, pair, 0)
    hat, norm_scale = moments(padded_rows(img_ref[...]))
    gain = vec_ref[0:1, :width]
    normed = (hat * gain + vec_ref[1:2, :width]).astype(BF16)
    grad_triple = gtrip[...]
    accw[...] += dot(normed.T, grad_triple)
    gtrip_ref[0:1] += jnp.sum(grad_triple.astype(F32), 0, keepdims=True)
    back = dot_nt(grad_triple, w_ref[...])
    accv[0:1] += jnp.sum(back * hat, 0, keepdims=True)
    accv[1:2] += jnp.sum(back, 0, keepdims=True)
    grad_in = gres_ref[...].reshape(rows, width) + norm_backward(back, hat, norm_scale, gain)
    gin_ref[...] = unpadded(grad_in, group).astype(BF16)

    @pl.when(step == pl.num_programs(0) - 1)
    def _():
        gw_ref[...] = accw[...]
        gvec_ref[...] = accv[...]
        gbias_ref[...] = accb[...]


def whole(shape):
    return pl.BlockSpec(shape, lambda *_: (0,) * len(shape))


def params(mib):
    return pltpu.CompilerParams(
        dimension_semantics=("arbitrary",), vmem_limit_bytes=mib * MIB
    )


def part_sizes(slots):
    group = 2 if slots % 2 == 0 else 1
    steps = slots // group
    calls = next(c for c in (3, 2, 1) if steps % c == 0)
    return group, steps // calls, calls


def attention_forward(images, w_qkv, vec, bias, heads, call, steps, group, carried):
    slots, width = images.shape[0], images.shape[-1]
    first = call * steps
    tokens = SIDE * COLS
    groups = width // LANES
    stack = bias.shape[1]
    block = lambda i: (first + i, 0, 0)
    block4 = lambda i: (first + i, 0, 0, 0)
    shapes = [
        jax.ShapeDtypeStruct((slots, tokens, 3 * width), BF16),
        jax.ShapeDtypeStruct((2 * slots, groups, stack, KEYS), BF16),
        jax.ShapeDtypeStruct((2 * slots, PAIR, width), BF16),
    ]
    flops = steps * group * tokens * width * width * 6 * 2
    return pl.pallas_call(
        partial(forward_kernel, heads),
        grid=(steps,),
        in_specs=[
            pl.BlockSpec((group, SIDE, SIDE, width), block4),
            whole(w_qkv.shape),
            whole(vec.shape),
            whole(bias.shape),
        ]
        + [pl.BlockSpec(memory_space=pl.ANY)] * len(carried),
        out_specs=[
            pl.BlockSpec((group, tokens, 3 * width), block),
            pl.BlockSpec((2 * group, groups, stack, KEYS), block4),
            pl.BlockSpec((2 * group, PAIR, width), block),
        ],
        out_shape=shapes,
        scratch_shapes=[pltpu.VMEM((group * tokens + COLS, 3 * width), BF16)],
        input_output_aliases={4 + i: i for i in range(len(carried))},
        compiler_params=params(56),
        cost_estimate=pl.CostEstimate(flops=flops, bytes_accessed=8 * MIB, transcendentals=0),
        name="attention_forward",
    )(images, w_qkv, vec, bias, *carried)


def feed_forward(counts, images, cotangent, mixed, w_proj, w1, w2, vec, b1):
    slots, width = images.shape[0], images.shape[-1]
    group = next(g for g in (4, 2, 1) if slots % g == 0)
    tokens = SIDE * COLS
    chunks, _, span = w1.shape
    image_spec = pl.BlockSpec((group, SIDE, SIDE, width), lambda i: (i, 0, 0, 0))
    row_spec = pl.BlockSpec((group, tokens, width), lambda i: (i, 0, 0))
    outs = [
        (images.shape, BF16, image_spec),
        ((slots, tokens, width), F32, row_spec),
        ((slots, tokens, width), BF16, row_spec),
    ] + [
        (shape, kind, whole(shape))
        for shape, kind in (
            (w1.shape, BF16),
            (w2.shape, BF16),
            (w_proj.shape, BF16),
            ((8, width), F32),
            ((chunks, 8, span), F32),
        )
    ]
    return pl.pallas_call(
        mlp_kernel,
        grid=(slots // group,),
        in_specs=[
            pl.BlockSpec(memory_space=pltpu.SMEM),
            image_spec,
            image_spec,
            row_spec,
            whole(w_proj.shape),
            whole(w1.shape),
            whole(w2.shape),
            whole(vec.shape),
            whole(b1.shape),
        ],
        out_specs=[o[2] for o in outs],
        out_shape=[jax.ShapeDtypeStruct(o[0], o[1]) for o in outs],
        scratch_shapes=[
            pltpu.VMEM(w1.shape, F32),
            pltpu.VMEM((chunks, width, span), F32),
            pltpu.VMEM(w_proj.shape, F32),
            pltpu.VMEM((8, width), F32),
            pltpu.VMEM((chunks, 8, span), F32),
        ],
        compiler_params=params(62),
        cost_estimate=pl.CostEstimate(
            flops=slots * tokens * width * (width * 3 + chunks * span * 6) * 2,
            bytes_accessed=32 * MIB,
            transcendentals=0,
        ),
        name="feed_forward",
    )(counts, images, cotangent, mixed, w_proj, w1, w2, vec, b1)


def attention_backward(
    images, gres, gmix, triple, probs, w_qkv, vec, heads, call, steps, group, carried
):
    slots, width = images.shape[0], images.shape[-1]
    first = call * steps
    tokens = SIDE * COLS
    groups, stack = probs.shape[1:3]
    block = lambda i: (first + i, 0, 0)
    block4 = lambda i: (first + i, 0, 0, 0)
    image_spec = pl.BlockSpec((group, SIDE, SIDE, width), block4)
    sums = [
        ((width, 3 * width), F32),
        ((8, width), F32),
        ((8, 3 * width), F32),
        ((groups, stack, KEYS), F32),
    ]
    return pl.pallas_call(
        partial(backward_kernel, heads),
        grid=(steps,),
        in_specs=[
            image_spec,
            pl.BlockSpec((group, tokens, width), block),
            pl.BlockSpec((2 * group, PAIR, width), block),
            pl.BlockSpec((group, tokens, 3 * width), block),
            pl.BlockSpec((2 * group, groups, stack, KEYS), block4),
            whole(w_qkv.shape),
            whole(vec.shape),
        ]
        + ([pl.BlockSpec(memory_space=pl.ANY)] + [whole(s) for s, _ in sums] if carried else []),
        out_specs=[image_spec] + [whole(s) for s, _ in sums],
        out_shape=[jax.ShapeDtypeStruct(images.shape, BF16)]
        + [jax.ShapeDtypeStruct(s, k) for s, k in sums],
        scratch_shapes=[
            pltpu.VMEM((group * tokens + COLS, 3 * width), BF16),
            pltpu.VMEM((group * tokens, 3 * width), BF16),
            pltpu.VMEM(sums[0][0], F32),
            pltpu.VMEM(sums[1][0], F32),
            pltpu.VMEM(sums[3][0], F32),
        ],
        input_output_aliases={7: 0} if carried else {},
        compiler_params=params(62),
        cost_estimate=pl.CostEstimate(
            flops=steps * group * tokens * width * width * 12 * 2,
            bytes_accessed=16 * MIB,
            transcendentals=0,
        ),
        name="attention_backward",
    )(images, gres, gmix, triple, probs, w_qkv, vec, *carried)


def flip(values, bit, devices):
    return lax.ppermute(values, "dev", [(i, i ^ bit) for i in range(devices)])


def bit_list(devices):
    return [1 << i for i in range(devices.bit_length() - 1)]


def has(me, bit):
    return (me & bit) != 0


def gather_blocks(block, me, devices, bits):
    held = block[None]
    for bit in bits:
        other = flip(held, bit, devices)
        low = jnp.where(has(me, bit), other, held)
        high = jnp.where(has(me, bit), held, other)
        held = jnp.stack([low, high], 1).reshape((-1,) + block.shape)
    return held


def scatter_sums(blocks, me, devices, order, exact_pairs=False):
    bits = bit_list(devices)
    left = bits[::-1]
    tail = blocks.shape[1:]
    held = blocks.reshape((2,) * len(bits) + tail)
    for bit in order:
        axis = left.index(bit)
        mine = has(me, bit).astype(jnp.int32)
        keep = lax.dynamic_index_in_dim(held, mine, axis, keepdims=False)
        send = lax.dynamic_index_in_dim(held, 1 - mine, axis, keepdims=False).astype(BF16)
        if exact_pairs:
            keep = keep.astype(BF16)
        held = keep.astype(F32) + flip(send, bit, devices).astype(F32)
        left.remove(bit)
    return held


def two_orders(devices):
    bits = bit_list(devices)
    if len(bits) < 3:
        return bits, bits
    return bits, [bits[0], bits[2], bits[1]] + bits[3:]


def window_places():
    picks = np.zeros((2, KEYS, WINDOW * WINDOW), np.float32)
    for r in range(WINDOW):
        for c in range(SIDE):
            picks[c // WINDOW, r * COLS + c, r * WINDOW + c % WINDOW] = 1.0
    return picks


def shards(
    devices,
    images,
    cotangent,
    image_counts,
    rel_index,
    ln1_gain,
    ln1_shift,
    w_qkv,
    q_bias,
    v_bias,
    w_proj,
    b_proj,
    ln2_gain,
    ln2_shift,
    w_fc1,
    b_fc1,
    w_fc2,
    b_fc2,
    bias_table,
):
    me = lax.axis_index("dev")
    slots, width = images.shape[0], images.shape[3]
    table_rows, heads = bias_table.shape
    own = ln1_gain.shape[0]
    span = b_fc1.shape[0]
    ff = span * devices
    chunks = ff // width
    bits = bit_list(devices)
    down = bits[::-1]
    order_one, order_two = two_orders(devices)

    vec_pad = -(4 * own) % width
    attn_block = jnp.concatenate(
        [
            w_qkv.reshape(own, 3, width).transpose(1, 0, 2).reshape(3 * own, width),
            jnp.pad(jnp.concatenate([ln1_gain, ln1_shift, q_bias, v_bias]), (0, vec_pad)).reshape(
                -1, width
            ),
        ]
    )
    attn_all = gather_blocks(attn_block, me, devices, down)
    qkv_full = (
        attn_all[:, : 3 * own]
        .reshape(devices, 3, own, width)
        .transpose(0, 2, 1, 3)
        .reshape(width, 3 * width)
    )
    vecs = attn_all[:, 3 * own :].reshape(devices, -1)[:, : 4 * own]
    vecs = vecs.reshape(devices, 4, own).transpose(1, 0, 2).reshape(4, width).astype(F32)
    row = lambda *parts: jnp.pad(jnp.concatenate(parts), (0, 3 * width - sum(p.shape[0] for p in parts)))
    zero = jnp.zeros((width,), F32)
    vec_one = jnp.stack([row(vecs[0]), row(vecs[1]), row(vecs[2], zero, vecs[3])])
    vec_one = jnp.pad(vec_one, ((0, 5), (0, 0)))

    mlp_vec = jnp.concatenate([b_proj, ln2_gain, ln2_shift, b_fc2, b_fc1])
    mlp_pad = -mlp_vec.shape[0] % width
    mlp_block = jnp.concatenate(
        [
            w_fc2,
            w_fc1.reshape(own, chunks, width).transpose(1, 0, 2).reshape(chunks * own, width),
            w_proj,
            jnp.pad(mlp_vec, (0, mlp_pad)).reshape(-1, width),
        ]
    )
    half = mlp_block.shape[0] // 2
    up_two = order_two[::-1]

    def gather_two(block):
        held = block[None]
        for bit in up_two:
            other = flip(held, bit, devices)
            low = jnp.where(has(me, bit), other, held)
            high = jnp.where(has(me, bit), held, other)
            held = jnp.stack([low, high], 1).reshape((-1,) + block.shape)
        shape = held.shape[1:]
        held = held.reshape((2,) * len(bits) + shape)
        axes = [up_two.index(b) for b in down]
        return held.transpose(axes + [len(bits) + i for i in range(len(shape))]).reshape(
            (devices,) + shape
        )

    mlp_all = jnp.concatenate(
        [gather_blocks(mlp_block[:half], me, devices, down), gather_two(mlp_block[half:])], 1
    )
    at = span
    w2_full = mlp_all[:, :span].reshape(chunks, width, width)
    w1_full = (
        mlp_all[:, at : at + chunks * own]
        .reshape(devices, chunks, own, width)
        .transpose(1, 0, 2, 3)
        .reshape(chunks, width, width)
    )
    at += chunks * own
    proj_full = mlp_all[:, at : at + own].reshape(width, width)
    at += own
    mlp_vecs = mlp_all[:, at:].reshape(devices, -1)
    vec_two = mlp_vecs[:, : 4 * own].reshape(devices, 4, own).transpose(1, 0, 2).reshape(4, width)
    vec_two = jnp.pad(vec_two.astype(F32), ((0, 4), (0, 0)))
    b1_full = mlp_vecs[:, 4 * own : 4 * own + span].reshape(chunks, 1, width).astype(F32)

    picks = window_places()
    index_low = rel_index.astype(BF16)
    places = sum(
        dot(dot(jnp.asarray(pick[:PAIR], BF16), index_low).astype(BF16), jnp.asarray(pick.T, BF16))
        for pick in picks
    )
    valid = jnp.asarray(sum(pick[:PAIR].sum(1)[:, None] * pick.sum(1)[None] for pick in picks) > 0)
    places = jnp.where(valid, places.astype(jnp.int32), -1)
    depth = -(-table_rows // LANES) * LANES
    selector = (places[:, :, None] == jnp.arange(depth, dtype=jnp.int32)).astype(BF16)
    selector = selector.reshape(PAIR * KEYS, depth)
    table = jnp.pad(bias_table, ((0, depth - table_rows), (0, 0))).T
    high = table.astype(BF16)
    mid = (table - high.astype(F32)).astype(BF16)
    low = (table - high.astype(F32) - mid.astype(F32)).astype(BF16)
    bias = dot_nt(jnp.concatenate([high, mid, low]), selector)
    bias = (bias[:heads] + bias[heads : 2 * heads] + bias[2 * heads :]).reshape(heads, PAIR, KEYS)
    bias = jnp.where(valid, bias, NEG)
    per = LANES // (width // heads)
    bias = bias.reshape(heads // per, per * PAIR, KEYS)

    group, steps, calls = part_sizes(slots)
    carried = ()
    for call in range(calls):
        carried = attention_forward(
            images, qkv_full, vec_one, bias, heads, call, steps, group, carried
        )
    triple, probs, mixed = carried
    output, gres, gmix, g1, g2, gp, gvec, gb1 = feed_forward(
        image_counts,
        images,
        cotangent,
        mixed.reshape(slots, SIDE * COLS, width),
        proj_full,
        w1_full,
        w2_full,
        vec_two,
        b1_full,
    )

    small = jnp.concatenate(
        [
            gvec[:4].reshape(4, devices, own).transpose(1, 0, 2).reshape(devices, 4 * own),
            gb1[:, 0].reshape(devices, span),
        ],
        1,
    )
    small = jnp.pad(small, ((0, 0), (0, mlp_pad))).astype(BF16).reshape(devices, -1, width)
    g1 = g1.reshape(chunks, devices, own, width).transpose(1, 0, 2, 3)
    mlp_sums = jnp.concatenate(
        [
            g2.reshape(devices, span, width),
            g1.reshape(devices, chunks * own, width),
            gp.reshape(devices, own, width),
            small,
        ],
        1,
    )
    mlp_mine = jnp.concatenate(
        [
            scatter_sums(mlp_sums[:, :half], me, devices, order_one),
            scatter_sums(mlp_sums[:, half:], me, devices, order_two),
        ]
    )
    grad_fc2 = mlp_mine[:span]
    at = span
    grad_fc1 = mlp_mine[at : at + chunks * own].reshape(chunks, own, width)
    grad_fc1 = grad_fc1.transpose(1, 0, 2).reshape(own, ff)
    at += chunks * own
    grad_proj = mlp_mine[at : at + own]
    mlp_small = mlp_mine[at + own :].reshape(-1)
    grad_proj_bias, grad_gain_two, grad_shift_two, grad_fc2_bias = (
        mlp_small[i * own : (i + 1) * own] for i in range(4)
    )
    grad_fc1_bias = mlp_small[4 * own : 4 * own + span]

    gmix = gmix.reshape(2 * slots, PAIR, width)
    carried = ()
    for call in range(calls):
        carried = attention_backward(
            images, gres, gmix, triple, probs, qkv_full, vec_one, heads, call, steps, group, carried
        )
    grad_input, gw, gvec, gtrip, gbias = carried

    gb = gbias.reshape(heads, PAIR * KEYS)
    gb_high = gb.astype(BF16)
    gb_low = (gb - gb_high.astype(F32)).astype(BF16)
    gtable = dot(jnp.concatenate([gb_high, gb_low]), selector)
    gtable = (gtable[:heads] + gtable[heads:])[:, :table_rows].reshape(-1)
    table_pad = -gtable.shape[0] % width
    gtable = jnp.pad(gtable, (0, table_pad)).astype(BF16).reshape(-1, width)
    small = jnp.stack(
        [gvec[0], gvec[1], gtrip[0, :width], gtrip[0, 2 * width :]]
    )
    small = small.reshape(4, devices, own).transpose(1, 0, 2).reshape(devices, 4 * own)
    small = jnp.pad(small, ((0, 0), (0, vec_pad))).astype(BF16).reshape(devices, -1, width)
    attn_sums = jnp.concatenate(
        [
            gw.astype(BF16).reshape(devices, own, 3, width).transpose(0, 2, 1, 3).reshape(devices, 3 * own, width),
            small,
            jnp.broadcast_to(gtable, (devices,) + gtable.shape),
        ],
        1,
    )
    half = attn_sums.shape[1] // 2
    one = scatter_sums(attn_sums[:, :half], me, devices, order_one)
    two = scatter_sums(attn_sums[:, half:], me, devices, order_two, True)
    mine = jnp.concatenate([one, two])
    grad_qkv = mine[: 3 * own].reshape(3, own, width).transpose(1, 0, 2).reshape(own, 3 * width)
    at = 3 * own
    vec_rows = small.shape[1]
    attn_small = mine[at : at + vec_rows].reshape(-1)
    grad_gain_one, grad_shift_one, grad_query_bias, grad_value_bias = (
        attn_small[i * own : (i + 1) * own] for i in range(4)
    )
    at += vec_rows
    table_total = mine[at:].reshape(-1)[: heads * table_rows].reshape(heads, table_rows).T
    return (
        output,
        grad_input,
        grad_gain_one,
        grad_shift_one,
        grad_qkv,
        grad_query_bias,
        grad_value_bias,
        grad_proj,
        grad_proj_bias,
        grad_gain_two,
        grad_shift_two,
        grad_fc1,
        grad_fc1_bias,
        grad_fc2,
        grad_fc2_bias,
        table_total,
    )


def solution(mesh):
    rows = P("dev", None)
    image = P("dev", None, None, None)
    flat = P("dev")
    in_specs = (
        image, image, flat, P(), flat, flat, rows, flat, flat, rows, flat,
        flat, flat, rows, flat, rows, flat, P(),
    )
    out_specs = (
        image, image, flat, flat, rows, flat, flat, rows, flat,
        flat, flat, rows, flat, rows, flat, P(),
    )
    body = partial(shards, mesh.shape["dev"])
    return jax.shard_map(body, mesh=mesh, in_specs=in_specs, out_specs=out_specs, check_vma=False)
```

```python
from functools import partial

import jax
import jax.numpy as jnp
import numpy as np
from jax import lax
from jax.experimental import pallas as pl
from jax.experimental.pallas import tpu as pltpu
from jax.sharding import PartitionSpec as P

WINDOW = 7
SIDE = 14
COLS = 16
PAIR = WINDOW * COLS
KEYS = 128
LANES = 128
EPSILON = 1e-05
HIGHEST = lax.Precision.HIGHEST
MIB = 2**20
NEG = -1e30
VEC_ROWS = 16
UNROLL = 4
F32 = jnp.float32
BF16 = jnp.bfloat16


def dot(left, right):
    return lax.dot_general(left, right, (((1,), (0,)), ((), ())), preferred_element_type=F32)


def dot_nt(left, right):
    return lax.dot_general(left, right, (((1,), (1,)), ((), ())), preferred_element_type=F32)


def dot_tn(left, right):
    return lax.dot_general(left, right, (((0,), (0,)), ((), ())), preferred_element_type=F32)


def pl_reciprocal(values):
    return pltpu.reciprocal(values, approx=True)


def padded_rows(block):
    wide = block.astype(F32)
    wide = jnp.pad(wide, ((0, 0), (0, 0), (0, COLS - SIDE), (0, 0)))
    return wide.reshape(-1, block.shape[-1])


def unpadded(rows, images):
    return rows.reshape(images, SIDE, COLS, rows.shape[-1])[:, :, :SIDE, :]


def moments(values):
    center = values - jnp.mean(values, -1, keepdims=True)
    spread = jnp.mean(center * center, -1, keepdims=True)
    scale = lax.rsqrt(spread + EPSILON)
    return center * scale, scale


def norm_backward(grad, hat, scale, gain):
    inner = grad * gain
    mean_one = jnp.mean(inner, -1, keepdims=True)
    mean_two = jnp.mean(inner * hat, -1, keepdims=True)
    return scale * (inner - mean_one - hat * mean_two)


def head_masks(head_dim):
    lane = lax.broadcasted_iota(jnp.int32, (1, LANES), 1) // head_dim
    return [lane == h for h in range(LANES // head_dim)]


def stacked(block, masks):
    zero = jnp.zeros_like(block)
    return jnp.concatenate([jnp.where(m, block, zero) for m in masks], 0)


def side_by_side(tall, parts):
    rows = tall.shape[0] // parts
    return jnp.concatenate([tall[i * rows : (i + 1) * rows] for i in range(parts)], 1)


def fetch(ids_ref, pieces, full, sems):
    copies = []
    for number, piece in enumerate(pieces):
        count = piece.shape[0]
        for j in range(count):
            at = number * count + j
            copies.append(
                pltpu.make_async_copy(piece.at[j], full.at[ids_ref[at]], sems.at[at])
            )
    return copies


def block_rows(full, start, rows):
    part = full[:, start : start + rows, :]
    return part.reshape(-1, part.shape[-1])


def vector_rows(full, start):
    return jnp.sum(full[:, start : start + VEC_ROWS, :].astype(F32), 0)


def forward_kernel(heads, carried, ids_ref, img_ref, one_ref, two_ref, bias_ref, *refs):
    triple_ref, probs_ref, mixed_ref, trip, full, vec, sems = refs[carried:]
    group = img_ref.shape[0]
    width = img_ref.shape[-1]
    head_dim = width // heads
    scale = head_dim ** (-0.5)
    per = LANES // head_dim
    rows = group * SIDE * COLS
    own = width // full.shape[0]

    @pl.when(pl.program_id(0) == 0)
    def _():
        copies = fetch(ids_ref, (one_ref, two_ref), full, sems)
        for copy in copies:
            copy.start()
        for copy in copies:
            copy.wait()
        vec[...] = vector_rows(full, 3 * own)

    inputs = padded_rows(img_ref[...])
    hat, _ = moments(inputs)
    normed = (hat * vec[0:1] + vec[1:2]).astype(BF16)
    trip[rows:, :] = jnp.zeros((COLS, 3 * width), BF16)
    for c, extra in enumerate((vec[2:3], None, vec[3:4])):
        part = dot(normed, block_rows(full, c * own, own))
        if extra is not None:
            part = part + extra
        part = part.astype(BF16)
        trip[0:rows, c * width : (c + 1) * width] = part
        triple_ref[:, :, c * width : (c + 1) * width] = part.reshape(group, SIDE * COLS, width)
    masks = head_masks(head_dim)

    def pair(p, carry):
        start = pl.multiple_of(p * PAIR, COLS)
        for g in range(width // LANES):
            q = trip[pl.ds(start, PAIR), g * LANES : (g + 1) * LANES]
            k = trip[pl.ds(start, KEYS), width + g * LANES : width + (g + 1) * LANES]
            v = trip[pl.ds(start, KEYS), 2 * width + g * LANES : 2 * width + (g + 1) * LANES]
            scores = dot_nt(stacked(q, masks), k) * scale + bias_ref[g]
            top = jnp.max(scores, -1, keepdims=True)
            raised = jnp.exp(scores - top)
            total = jnp.sum(raised, -1, keepdims=True)
            probs = (raised * (1.0 / total)).astype(BF16)
            probs_ref[p, g] = probs
            mixed = dot(side_by_side(probs, per), stacked(v, masks))
            mixed_ref[p, :, g * LANES : (g + 1) * LANES] = mixed.astype(BF16)
        return carry

    lax.fori_loop(0, 2 * group, pair, 0, unroll=UNROLL)


def mlp_kernel(
    ids_ref, counts_ref, img_ref, cot_ref, mixed_ref, one_ref, two_ref,
    out_ref, gres_ref, gmix_ref, keep_ref, send_ref,
    full, vec, acc1, acc2, accp, accv, accb, turned, sems,
):
    step = pl.program_id(0)
    group = img_ref.shape[0]
    width = img_ref.shape[-1]
    rows = group * SIDE * COLS
    chunks = acc1.shape[0]
    owners = full.shape[0]
    own = width // owners
    span = chunks * own
    at_one, at_proj, at_vec = span, 2 * span, 2 * span + own

    @pl.when(step == 0)
    def _():
        copies = fetch(ids_ref, (one_ref, two_ref), full, sems)
        for copy in copies:
            copy.start()
        for ref in (acc1, acc2, accp, accv, accb):
            ref[...] = jnp.zeros_like(ref)
        for copy in copies:
            copy.wait()
        vec[...] = vector_rows(full, at_vec)

    row = lax.broadcasted_iota(jnp.int32, (rows, 1), 0)
    image = row // (SIDE * COLS)
    live = ((step * group + image) < counts_ref[0]) & (row % COLS < SIDE)
    mixed = mixed_ref[...].reshape(rows, width)
    w_proj = block_rows(full, at_proj, own)
    residual = padded_rows(img_ref[...]) + dot(mixed, w_proj) + vec[0:1]
    hat, scale = moments(residual)
    gain = vec[1:2]
    normed = (hat * gain + vec[2:3]).astype(BF16)
    normed_t = normed.T
    grad_out = jnp.where(live, padded_rows(cot_ref[...]), 0.0)
    grad_low = grad_out.astype(BF16)
    grad_low_t = grad_low.T
    total, back = None, None
    for c in range(chunks):
        w1 = block_rows(full, at_one + c * own, own)
        half = owners // chunks
        w2 = full[c * half : (c + 1) * half, :span, :].reshape(width, width)
        hidden = dot(normed, w1) + vec[4 + c : 5 + c]
        size = jnp.abs(hidden)
        bell = jnp.exp(-0.5 * hidden * hidden)
        t = pl_reciprocal(1.0 + (0.3275911 * 0.7071067811865476) * size)
        poly = t * (
            0.127414796
            + t * (-0.142248368 + t * (0.7107068705 + t * (-0.7265760135 + t * 0.5307027145)))
        )
        tail = poly * bell
        below = jnp.where(hidden < 0, tail, 1.0 - tail)
        act = (hidden * below).astype(BF16)
        slope = below + hidden * (0.3989422804014327 * bell)
        after = dot(act, w2)
        total = after if total is None else total + after
        grad_hidden = (slope * dot_nt(grad_low, w2)).astype(BF16)
        before = dot_nt(grad_hidden, w1)
        back = before if back is None else back + before
        acc1[c] += dot(normed_t, grad_hidden)
        acc2[c] += dot(grad_low_t, act)
        accb[c : c + 1] += jnp.sum(grad_hidden.astype(F32), 0, keepdims=True)
    result = jnp.where(live, residual + total + vec[3:4], 0.0)
    out_ref[...] = unpadded(result, group).astype(BF16)
    grad_res = grad_out + norm_backward(back, hat, scale, gain)
    gres_ref[...] = grad_res.reshape(group, SIDE * COLS, width)
    grad_res_low = grad_res.astype(BF16)
    gmix_ref[...] = dot_nt(grad_res_low, w_proj).astype(BF16).reshape(group, SIDE * COLS, width)
    accp[...] += dot(mixed.T, grad_res_low)
    accv[0:1] += jnp.sum(grad_res_low.astype(F32), 0, keepdims=True)
    accv[1:2] += jnp.sum(back * hat, 0, keepdims=True)
    accv[2:3] += jnp.sum(back, 0, keepdims=True)
    accv[3:4] += jnp.sum(grad_low.astype(F32), 0, keepdims=True)

    @pl.when(step == pl.num_programs(0) - 1)
    def _():
        for c in range(chunks):
            turned[c * width : (c + 1) * width] = acc2[c].astype(BF16).T
        sums = jnp.concatenate([accv[0:4], accb[0:4], jnp.zeros((8, width), F32)], 0).astype(BF16)
        half = owners // 2
        for number, ref in enumerate((keep_ref, send_ref)):

            def place(j, carry, ref=ref, number=number):
                owner = ids_ref[number * half + j]
                ref[j, 0:span] = turned[pl.ds(pl.multiple_of(owner * span, span), span)]
                mine = pl.ds(pl.multiple_of(owner * own, own), own)
                for c in range(chunks):
                    ref[j, at_one + c * own : at_one + (c + 1) * own] = acc1[c, mine].astype(BF16)
                ref[j, at_proj : at_proj + own] = accp[mine].astype(BF16)
                ref[j, at_vec : at_vec + VEC_ROWS] = sums
                return carry

            lax.fori_loop(0, half, place, 0)


def backward_kernel(
    heads, first, last, ids_ref, img_ref, gres_ref, gmix_ref, triple_ref, probs_ref, one_ref,
    two_ref, choice_ref, *refs
):
    trip, gtrip, full, vec, sems = refs[-5:]
    step = pl.program_id(0)
    group = img_ref.shape[0]
    width = img_ref.shape[-1]
    head_dim = width // heads
    scale = head_dim ** (-0.5)
    per = LANES // head_dim
    rows = group * SIDE * COLS
    own = width // full.shape[0]
    carried = () if first else refs[1:4]
    outs = refs[0 if first else 4 : -5]
    gin_ref = outs[0]
    if last:
        keep_ref, send_ref, accw, accv, accb = outs[1:]
    else:
        accw, accv, accb = outs[1:]
    copies = fetch(ids_ref, (one_ref, two_ref), full, sems)

    @pl.when(step == 0)
    def _():
        for copy in copies:
            copy.start()
        if carried:
            accw[...] = carried[0][...]
            accv[...] = carried[1][...]
            accb[...] = carried[2][...]
        else:
            accw[...] = jnp.zeros_like(accw)
            accv[...] = jnp.zeros_like(accv)
            accb[...] = jnp.zeros_like(accb)

    trip[0:rows, :] = triple_ref[...].reshape(rows, 3 * width)
    trip[rows:, :] = jnp.zeros((COLS, 3 * width), BF16)
    masks = head_masks(head_dim)

    def pair(p, carry):
        start = pl.multiple_of(p * PAIR, COLS)
        for g in range(width // LANES):
            lo, hi = g * LANES, (g + 1) * LANES
            q = trip[pl.ds(start, PAIR), lo:hi]
            k = trip[pl.ds(start, KEYS), width + lo : width + hi]
            v = trip[pl.ds(start, KEYS), 2 * width + lo : 2 * width + hi]
            probs = probs_ref[p, g]
            grad_mixed = stacked(gmix_ref[p, :, lo:hi], masks)
            wide = probs.astype(F32)
            grad_probs = dot_nt(grad_mixed, v)
            inner = jnp.sum(wide * grad_probs, -1, keepdims=True)
            grad_scores = (wide * (grad_probs - inner)).astype(BF16)
            accb[g] += grad_scores.astype(F32)
            grad_q = dot(side_by_side(grad_scores, per), stacked(k, masks)) * scale
            grad_k = dot_tn(grad_scores, stacked(q, masks)) * scale
            grad_v = dot_tn(probs, grad_mixed)
            gtrip[pl.ds(start, PAIR), lo:hi] = grad_q.astype(BF16)
            gtrip[pl.ds(start, PAIR), width + lo : width + hi] = grad_k[:PAIR].astype(BF16)
            gtrip[pl.ds(start, PAIR), 2 * width + lo : 2 * width + hi] = grad_v[:PAIR].astype(BF16)
        return carry

    lax.fori_loop(0, 2 * group, pair, 0, unroll=UNROLL)

    @pl.when(step == 0)
    def _():
        for copy in copies:
            copy.wait()
        vec[...] = vector_rows(full, 3 * own)

    hat, norm_scale = moments(padded_rows(img_ref[...]))
    gain = vec[0:1]
    normed_t = (hat * gain + vec[1:2]).astype(BF16).T
    back = None
    for c in range(3):
        part = gtrip[:, c * width : (c + 1) * width]
        accw[c] += dot(normed_t, part)
        accv[2 + c : 3 + c] += jnp.sum(part.astype(F32), 0, keepdims=True)
        before = dot_nt(part, block_rows(full, c * own, own))
        back = before if back is None else back + before
    accv[0:1] += jnp.sum(back * hat, 0, keepdims=True)
    accv[1:2] += jnp.sum(back, 0, keepdims=True)
    grad_in = gres_ref[...].reshape(rows, width) + norm_backward(back, hat, norm_scale, gain)
    gin_ref[...] = unpadded(grad_in, group).astype(BF16)

    if last:

        @pl.when(step == pl.num_programs(0) - 1)
        def _():
            query = lax.broadcasted_iota(jnp.int32, (PAIR, PAIR), 0)
            other = lax.broadcasted_iota(jnp.int32, (PAIR, PAIR), 1)
            turn = jnp.where(query + other == PAIR - 1, 1.0, 0.0).astype(BF16)
            sums = []
            for h in range(heads):
                tile = accb[h // per, h % per * PAIR : (h % per + 1) * PAIR]
                high = tile.astype(BF16)
                low = (tile - high.astype(F32)).astype(BF16)
                back_to_front = dot(turn, jnp.concatenate([high, low], 1))
                back_to_front = back_to_front[:, :KEYS] + back_to_front[:, KEYS:]
                wide = jnp.concatenate([back_to_front, jnp.zeros_like(back_to_front)], 1)
                skewed = pltpu.roll(wide, 0, 1, stride=1, stride_axis=0)
                sums.append(jnp.sum(skewed, 0, keepdims=True))
            sums = pltpu.roll(jnp.concatenate(sums, 0), 2 * KEYS - PAIR + 1, 1)
            high = sums.astype(BF16)
            low = (sums - high.astype(F32)).astype(BF16)
            table = dot(high, choice_ref[...]) + dot(low, choice_ref[...])
            pieces = width // LANES
            vectors = jnp.concatenate(
                [
                    accv[v : v + 1, i * LANES : (i + 1) * LANES]
                    for v in (0, 1, 2, 4)
                    for i in range(pieces)
                ],
                0,
            )
            rest = width - table.shape[1] - LANES
            tile = jnp.concatenate([table, vectors, jnp.zeros((VEC_ROWS, rest), F32)], 1).astype(BF16)
            half = full.shape[0] // 2
            for number, ref in enumerate((keep_ref, send_ref)):

                def place(j, carry, ref=ref, number=number):
                    owner = ids_ref[number * half + j]
                    mine = pl.ds(pl.multiple_of(owner * own, own), own)
                    for c in range(3):
                        ref[j, c * own : (c + 1) * own] = accw[c, mine].astype(BF16)
                    ref[j, 3 * own : 3 * own + VEC_ROWS] = tile
                    return carry

                lax.fori_loop(0, half, place, 0)


def bias_kernel(table_ref, seen_ref, bias_ref):
    heads = table_ref.shape[0]
    per = bias_ref.shape[1] // PAIR
    for h in range(heads):
        row = jnp.broadcast_to(table_ref[h : h + 1], (PAIR, table_ref.shape[1]))
        skewed = pltpu.roll(row, 0, 1, stride=1, stride_axis=0)
        at = h % per * PAIR
        bias_ref[h // per, at : at + PAIR] = jnp.where(seen_ref[...] > 0, skewed[:, :KEYS], NEG)


def whole(shape):
    return pl.BlockSpec(shape, lambda *_: (0,) * len(shape))


def params(mib):
    return pltpu.CompilerParams(
        dimension_semantics=("arbitrary",), vmem_limit_bytes=mib * MIB
    )


def image_group(slots):
    return 2 if slots % 2 == 0 else 1


def split_steps(steps, shares):
    if steps < 2 * len(shares):
        return [steps]
    sizes = [max(1, int(steps * share + 0.5)) for share in shares[:-1]]
    return sizes + [steps - sum(sizes)]


ANY = pl.BlockSpec(memory_space=pl.ANY)
SMEM = pl.BlockSpec(memory_space=pltpu.SMEM)


def weight_scratch(pieces):
    owners = 2 * pieces[0].shape[0]
    shape = (owners,) + pieces[0].shape[1:]
    return [
        pltpu.VMEM(shape, BF16),
        pltpu.VMEM((VEC_ROWS, shape[-1]), F32),
    ], pltpu.SemaphoreType.DMA((owners,))


def attention_forward(ids, images, pieces, bias, heads, first, steps, group, carried):
    slots, width = images.shape[0], images.shape[-1]
    tokens = SIDE * COLS
    groups, stack = bias.shape[:2]
    block = lambda i: (first + i, 0, 0)
    block4 = lambda i: (first + i, 0, 0, 0)
    full, sems = weight_scratch(pieces)
    return pl.pallas_call(
        partial(forward_kernel, heads, len(carried)),
        grid=(steps,),
        in_specs=[
            SMEM,
            pl.BlockSpec((group, SIDE, SIDE, width), block4),
            ANY,
            ANY,
            whole(bias.shape),
        ]
        + [ANY] * len(carried),
        out_specs=[
            pl.BlockSpec((group, tokens, 3 * width), block),
            pl.BlockSpec((2 * group, groups, stack, KEYS), block4),
            pl.BlockSpec((2 * group, PAIR, width), block),
        ],
        out_shape=[
            jax.ShapeDtypeStruct((slots, tokens, 3 * width), BF16),
            jax.ShapeDtypeStruct((2 * slots, groups, stack, KEYS), BF16),
            jax.ShapeDtypeStruct((2 * slots, PAIR, width), BF16),
        ],
        scratch_shapes=[pltpu.VMEM((group * tokens + COLS, 3 * width), BF16), *full, sems],
        input_output_aliases={5 + i: i for i in range(len(carried))},
        compiler_params=params(56),
        cost_estimate=pl.CostEstimate(
            flops=steps * group * tokens * width * width * 12,
            bytes_accessed=steps * group * 2 * MIB,
            transcendentals=0,
        ),
        name="attention_forward",
    )(ids, images, *pieces, bias, *carried)


def feed_forward(ids, counts, images, cotangent, mixed, pieces, chunks):
    slots, width = images.shape[0], images.shape[-1]
    group = next(g for g in (4, 2, 1) if slots % g == 0)
    tokens = SIDE * COLS
    image_spec = pl.BlockSpec((group, SIDE, SIDE, width), lambda i: (i, 0, 0, 0))
    row_spec = pl.BlockSpec((group, tokens, width), lambda i: (i, 0, 0))
    half = pieces[0].shape
    outs = [
        (images.shape, BF16, image_spec),
        ((slots, tokens, width), F32, row_spec),
        ((slots, tokens, width), BF16, row_spec),
        (half, BF16, whole(half)),
        (half, BF16, whole(half)),
    ]
    full, sems = weight_scratch(pieces)
    return pl.pallas_call(
        mlp_kernel,
        grid=(slots // group,),
        in_specs=[SMEM, SMEM, image_spec, image_spec, row_spec, ANY, ANY],
        out_specs=[o[2] for o in outs],
        out_shape=[jax.ShapeDtypeStruct(o[0], o[1]) for o in outs],
        scratch_shapes=[
            *full,
            pltpu.VMEM((chunks, width, width), F32),
            pltpu.VMEM((chunks, width, width), F32),
            pltpu.VMEM((width, width), F32),
            pltpu.VMEM((8, width), F32),
            pltpu.VMEM((8, width), F32),
            pltpu.VMEM((chunks * width, width), BF16),
            sems,
        ],
        compiler_params=params(62),
        cost_estimate=pl.CostEstimate(
            flops=slots * tokens * width * width * (3 + chunks * 6) * 2,
            bytes_accessed=32 * MIB,
            transcendentals=0,
        ),
        name="feed_forward",
    )(ids, counts, images, cotangent, mixed, *pieces)


def attention_backward(
    ids, images, gres, gmix, triple, probs, pieces, choice, heads, first, steps, group, carried, last
):
    slots, width = images.shape[0], images.shape[-1]
    tokens = SIDE * COLS
    groups, stack = probs.shape[1:3]
    block = lambda i: (first + i, 0, 0)
    block4 = lambda i: (first + i, 0, 0, 0)
    image_spec = pl.BlockSpec((group, SIDE, SIDE, width), block4)
    sums = [(3, width, width), (8, width), (groups, stack, KEYS)]
    half = pieces[0].shape
    outs = [(s, F32) for s in sums] if not last else [(half, BF16), (half, BF16)]
    full, sems = weight_scratch(pieces)
    return pl.pallas_call(
        partial(backward_kernel, heads, not carried, last),
        grid=(steps,),
        in_specs=[
            SMEM,
            image_spec,
            pl.BlockSpec((group, tokens, width), block),
            pl.BlockSpec((2 * group, PAIR, width), block),
            pl.BlockSpec((group, tokens, 3 * width), block),
            pl.BlockSpec((2 * group, groups, stack, KEYS), block4),
            ANY,
            ANY,
            whole(choice.shape),
        ]
        + ([ANY] + [whole(s) for s in sums] if carried else []),
        out_specs=[image_spec] + [whole(s) for s, _ in outs],
        out_shape=[jax.ShapeDtypeStruct(images.shape, BF16)]
        + [jax.ShapeDtypeStruct(s, k) for s, k in outs],
        scratch_shapes=([pltpu.VMEM(s, F32) for s in sums] if last else [])
        + [
            pltpu.VMEM((group * tokens + COLS, 3 * width), BF16),
            pltpu.VMEM((group * tokens, 3 * width), BF16),
            *full,
            sems,
        ],
        input_output_aliases={9: 0} if carried else {},
        compiler_params=params(62),
        cost_estimate=pl.CostEstimate(
            flops=steps * group * tokens * width * width * 24,
            bytes_accessed=steps * group * 4 * MIB,
            transcendentals=0,
        ),
        name="attention_backward",
    )(ids, images, gres, gmix, triple, probs, *pieces, choice, *carried)


def expand_bias(table, seen, heads, per):
    return pl.pallas_call(
        bias_kernel,
        out_shape=jax.ShapeDtypeStruct((heads // per, per * PAIR, KEYS), F32),
        name="expand_bias",
    )(table, seen)


def flip(values, bits, devices):
    return lax.ppermute(values, "dev", [(i, i ^ bits) for i in range(devices)])


def exchange_groups(devices):
    bits = [1 << i for i in range(devices.bit_length() - 1)]
    return [bits[:1]] + [bits[i : i + 2] for i in range(1, len(bits), 2)]


def mixes(group):
    found = [0]
    for bit in group:
        found = found + [f ^ bit for f in found]
    return found


def block_order(devices):
    order = [0]
    for group in exchange_groups(devices)[:0:-1]:
        order = [m ^ o for m in mixes(group) for o in order]
    return order + [exchange_groups(devices)[0][0] ^ o for o in order]


def gather_group(held, group, devices):
    return jnp.concatenate([held] + [flip(held, m, devices) for m in mixes(group)[1:]])


def add_group(held, group, devices):
    parts = jnp.split(held, 2 ** len(group))
    sums = [parts[0].astype(F32)]
    sums += [
        flip(part, m, devices).astype(F32) for part, m in zip(parts[1:], mixes(group)[1:])
    ]
    while len(sums) > 1:
        sums = [a + b for a, b in zip(sums[::2], sums[1::2])]
    return sums[0]


def tie(first, second):
    return lax.optimization_barrier((first, second))


def offsets():
    picks = np.full((2 * KEYS,), -1, np.int64)
    area = WINDOW * WINDOW
    for i in range(area):
        for j in range(area):
            place = (j // WINDOW - i // WINDOW) * COLS + j % WINDOW - i % WINDOW
            picks[place % (2 * KEYS)] = i * area + j
    return picks


def seen_keys():
    place = np.arange(KEYS)
    row, col = place // COLS, place % COLS
    side = np.where(col < SIDE, col // WINDOW, 2)
    ok = (row < WINDOW) & (side < 2)
    seen = (side[:PAIR, None] == side[None]) & ok[:PAIR, None] & ok[None]
    return seen.astype(np.float32)


def owner_lanes(vectors, me, devices):
    share = vectors.shape[-1]
    lane = lax.broadcasted_iota(jnp.int32, (1, share * devices), 1)
    return jnp.where(lane // share == me, jnp.tile(vectors, (1, devices)), 0)


def regroup(pieces, order, fields, me, devices, owners):
    by_number = np.argsort(np.array(order))
    blocks = jnp.concatenate(pieces)
    blocks = jnp.take(blocks, jnp.asarray(by_number)[jnp.arange(devices) ^ me], axis=0)
    out, at = [], 0
    for rows in fields:
        out.append(blocks[:, at : at + rows].reshape(owners, -1, blocks.shape[-1]))
        at += rows
    vectors = blocks[:, at:].reshape(owners, devices // owners, VEC_ROWS, -1)
    out.append(jnp.sum(vectors.astype(F32), 1).astype(BF16))
    return jnp.split(jnp.concatenate(out, 1), 2)


def ungroup(pieces, order, fields, me, devices, owners):
    blocks = jnp.concatenate(pieces)
    many = devices // owners
    out, at = [], 0
    for rows in fields:
        rows = rows * many
        out.append(blocks[:, at : at + rows].reshape(devices, rows // many, -1))
        at += rows
    out.append(jnp.repeat(blocks[:, at:], many, axis=0))
    blocks = jnp.take(jnp.concatenate(out, 1), jnp.asarray(np.array(order)) ^ me, axis=0)
    return jnp.split(blocks, 2)


def shards(
    devices,
    images,
    cotangent,
    image_counts,
    rel_index,
    ln1_gain,
    ln1_shift,
    w_qkv,
    q_bias,
    v_bias,
    w_proj,
    b_proj,
    ln2_gain,
    ln2_shift,
    w_fc1,
    b_fc1,
    w_fc2,
    b_fc2,
    bias_table,
):
    me = lax.axis_index("dev")
    slots, width = images.shape[0], images.shape[3]
    table_rows, heads = bias_table.shape
    own = ln1_gain.shape[0]
    span = b_fc1.shape[0]
    chunks = span // own
    per = LANES // (width // heads)
    groups = exchange_groups(devices)
    order = block_order(devices)
    aligned = own % COLS == 0
    owners = devices if aligned else width // COLS
    attn_fields = [own] * 3
    mlp_fields = [span] + [own] * (chunks + 1)
    if aligned:
        ids = jnp.asarray(np.array(order, np.int32)) ^ me
    else:
        ids = jnp.arange(owners, dtype=jnp.int32)

    attn_vec = owner_lanes(jnp.stack([ln1_gain, ln1_shift, q_bias, v_bias]), me, devices)
    attn_block = jnp.concatenate(
        [w_qkv[:, c * width : (c + 1) * width] for c in range(3)]
        + [attn_vec, jnp.zeros((VEC_ROWS - 4, width), BF16)]
    )
    mlp_vec = owner_lanes(jnp.stack([b_proj, ln2_gain, ln2_shift, b_fc2]), me, devices)
    hidden_vec = owner_lanes(b_fc1[None], me, devices).reshape(chunks, width)
    mlp_block = jnp.concatenate(
        [w_fc2]
        + [w_fc1[:, c * width : (c + 1) * width] for c in range(chunks)]
        + [w_proj, mlp_vec, hidden_vec, jnp.zeros((VEC_ROWS - 4 - chunks, width), BF16)]
    )
    picks = offsets()
    rows_of = rel_index.reshape(-1)[np.maximum(picks, 0)]
    rows_of = jnp.where(jnp.asarray(picks) >= 0, rows_of, -1)
    choice = (rows_of[:, None] == jnp.arange(2 * KEYS, dtype=jnp.int32)).astype(BF16)
    table = jnp.pad(bias_table, ((0, 2 * KEYS - table_rows), (0, 0))).T
    high = table.astype(BF16)
    mid = (table - high.astype(F32)).astype(BF16)
    low = (table - high.astype(F32) - mid.astype(F32)).astype(BF16)
    by_offset = dot_nt(jnp.concatenate([high, mid, low]), choice)
    by_offset = by_offset[:heads] + by_offset[heads : 2 * heads] + by_offset[2 * heads :]
    bias = expand_bias(by_offset, jnp.asarray(seen_keys()), heads, per)

    attn_held, mlp_held = attn_block[None], mlp_block[None]
    far = groups[:0:-1]
    for number, bits in enumerate(far):
        attn_held = gather_group(attn_held, bits, devices)
        attn_held, mlp_held = tie(attn_held, mlp_held)
        if number < len(far) - 1:
            mlp_held = gather_group(mlp_held, bits, devices)
    bias, attn_held = tie(bias, attn_held)
    attn_pieces = (attn_held, flip(attn_held, groups[0][0], devices))
    if not aligned:
        attn_pieces = regroup(attn_pieces, order, attn_fields, me, devices, owners)

    group = image_group(slots)
    sizes = split_steps(slots // group, (5 / 6, 1 / 6))
    mlp_held = gather_group(mlp_held, far[-1], devices)
    carried, first = (), 0
    for call, steps in enumerate(sizes):
        call_ids = ids
        if call > 0:
            call_ids, mlp_held = tie(ids, mlp_held)
        carried = attention_forward(
            call_ids, images, attn_pieces, bias, heads, first, steps, group, carried
        )
        first += steps
    triple, probs, mixed = carried
    mlp_pieces = (mlp_held, flip(mlp_held, groups[0][0], devices))
    if not aligned:
        mlp_pieces = regroup(mlp_pieces, order, mlp_fields, me, devices, owners)
    output, gres, gmix, *mlp_sums = feed_forward(
        ids,
        image_counts,
        images,
        cotangent,
        mixed.reshape(slots, SIDE * COLS, width),
        mlp_pieces,
        chunks,
    )

    if not aligned:
        mlp_sums = ungroup(mlp_sums, order, mlp_fields, me, devices, owners)
    gmix = gmix.reshape(2 * slots, PAIR, width)
    sizes = split_steps(slots // group, (1 / 6, 1 / 2, 1 / 3))
    stages = [groups[0]] + groups[1:]
    mlp_mine = None
    carried, first = (), 0
    for call, steps in enumerate(sizes):
        call_ids = ids
        if call == 1:
            moved = flip(mlp_sums[1], groups[0][0], devices)
            mlp_mine = (mlp_sums[0].astype(F32) + moved.astype(F32)).astype(BF16)
            call_ids, mlp_mine = tie(ids, mlp_mine)
        elif call == 2:
            mlp_mine = add_group(mlp_mine, groups[1], devices).astype(BF16)
            call_ids, mlp_mine = tie(ids, mlp_mine)
        carried = attention_backward(
            call_ids, images, gres, gmix, triple, probs, attn_pieces, choice, heads, first, steps,
            group, carried, call == len(sizes) - 1,
        )
        first += steps
    done = len(sizes)
    if done == 1:
        moved = flip(mlp_sums[1], groups[0][0], devices)
        mlp_mine = (mlp_sums[0].astype(F32) + moved.astype(F32)).astype(BF16)
    for bits in groups[1 if done == 1 else done - 1 :]:
        mlp_mine = add_group(mlp_mine.astype(BF16), bits, devices)
    mlp_mine = mlp_mine.reshape(-1, width).astype(F32)
    grad_fc2 = mlp_mine[:span]
    at = span
    grad_fc1 = jnp.concatenate(
        [mlp_mine[at + c * own : at + (c + 1) * own] for c in range(chunks)], 1
    )
    at += chunks * own
    grad_proj = mlp_mine[at : at + own]
    at += own
    vectors = lax.dynamic_slice_in_dim(mlp_mine[at : at + 4], me * own, own, 1)
    grad_proj_bias, grad_gain_two, grad_shift_two, grad_fc2_bias = vectors
    grad_fc1_bias = lax.dynamic_slice_in_dim(
        mlp_mine[at + 4 : at + 4 + chunks].reshape(-1), me * span, span, 0
    )

    grad_input, *attn_sums = carried
    if not aligned:
        attn_sums = ungroup(attn_sums, order, attn_fields, me, devices, owners)
    mine = attn_sums[0].astype(F32) + flip(attn_sums[1], groups[0][0], devices).astype(F32)
    for bits in groups[1:]:
        mine = add_group(mine.astype(BF16), bits, devices)
    mine = mine.reshape(-1, width)
    grad_qkv = jnp.concatenate([mine[c * own : (c + 1) * own] for c in range(3)], 1)
    tile = mine[3 * own :]
    table_total = tile[:heads, :table_rows].T
    vectors = tile[:, 2 * KEYS : 2 * KEYS + LANES].reshape(4, width)
    vectors = lax.dynamic_slice_in_dim(vectors, me * own, own, 1)
    grad_gain_one, grad_shift_one, grad_query_bias, grad_value_bias = vectors
    return (
        output,
        grad_input,
        grad_gain_one,
        grad_shift_one,
        grad_qkv,
        grad_query_bias,
        grad_value_bias,
        grad_proj,
        grad_proj_bias,
        grad_gain_two,
        grad_shift_two,
        grad_fc1,
        grad_fc1_bias,
        grad_fc2,
        grad_fc2_bias,
        table_total,
    )


def solution(mesh):
    rows = P("dev", None)
    image = P("dev", None, None, None)
    flat = P("dev")
    in_specs = (
        image, image, flat, P(), flat, flat, rows, flat, flat, rows, flat,
        flat, flat, rows, flat, rows, flat, P(),
    )
    out_specs = (
        image, image, flat, flat, rows, flat, flat, rows, flat,
        flat, flat, rows, flat, rows, flat, P(),
    )
    body = partial(shards, mesh.shape["dev"])
    return jax.shard_map(body, mesh=mesh, in_specs=in_specs, out_specs=out_specs, check_vma=False)
```

```python
from functools import partial

import jax
import jax.numpy as jnp
import numpy as np
from jax import lax
from jax.experimental import pallas as pl
from jax.experimental.pallas import tpu as pltpu
from jax.sharding import PartitionSpec as P

WINDOW = 7
SIDE = 14
COLS = 16
PAIR = WINDOW * COLS
KEYS = 128
LANES = 128
EPSILON = 1e-05
HIGHEST = lax.Precision.HIGHEST
MIB = 2**20
NEG = -1e30
VEC_ROWS = 16
UNROLL = 4
F32 = jnp.float32
BF16 = jnp.bfloat16


def dot(left, right):
    return lax.dot_general(left, right, (((1,), (0,)), ((), ())), preferred_element_type=F32)


def dot_nt(left, right):
    return lax.dot_general(left, right, (((1,), (1,)), ((), ())), preferred_element_type=F32)


def dot_tn(left, right):
    return lax.dot_general(left, right, (((0,), (0,)), ((), ())), preferred_element_type=F32)


def padded_rows(block):
    wide = block.astype(F32)
    wide = jnp.pad(wide, ((0, 0), (0, 0), (0, COLS - SIDE), (0, 0)))
    return wide.reshape(-1, block.shape[-1])


def unpadded(rows, images):
    return rows.reshape(images, SIDE, COLS, rows.shape[-1])[:, :, :SIDE, :]


def moments(values):
    center = values - jnp.mean(values, -1, keepdims=True)
    spread = jnp.mean(center * center, -1, keepdims=True)
    scale = lax.rsqrt(spread + EPSILON)
    return center * scale, scale


def norm_backward(grad, hat, scale, gain):
    inner = grad * gain
    mean_one = jnp.mean(inner, -1, keepdims=True)
    mean_two = jnp.mean(inner * hat, -1, keepdims=True)
    return scale * (inner - mean_one - hat * mean_two)


def head_masks(head_dim):
    lane = lax.broadcasted_iota(jnp.int32, (1, LANES), 1) // head_dim
    return [lane == h for h in range(LANES // head_dim)]


def stacked(block, masks):
    zero = jnp.zeros_like(block)
    return jnp.concatenate([jnp.where(m, block, zero) for m in masks], 0)


def side_by_side(tall, parts):
    rows = tall.shape[0] // parts
    return jnp.concatenate([tall[i * rows : (i + 1) * rows] for i in range(parts)], 1)


def fetch(ids_ref, pieces, full, sems):
    copies = []
    for number, piece in enumerate(pieces):
        count = piece.shape[0]
        for j in range(count):
            at = number * count + j
            copies.append(
                pltpu.make_async_copy(piece.at[j], full.at[ids_ref[at]], sems.at[at])
            )
    return copies


def block_rows(full, start, rows):
    part = full[:, start : start + rows, :]
    return part.reshape(-1, part.shape[-1])


def vector_rows(full, start):
    return jnp.sum(full[:, start : start + VEC_ROWS, :].astype(F32), 0)


def own_blocks(products, parts):
    rows, lanes = products.shape[0] // parts, products.shape[1] // parts
    return jnp.concatenate(
        [products[i * rows : (i + 1) * rows, i * lanes : (i + 1) * lanes] for i in range(parts)], 0
    )


def forward_kernel(heads, carried, ids_ref, img_ref, one_ref, two_ref, bias_ref, *refs):
    triple_ref, raised_ref, mixed_ref, inverse_ref, trip, full, vec, sems = refs[carried:]
    group = img_ref.shape[0]
    width = img_ref.shape[-1]
    head_dim = width // heads
    scale = head_dim ** (-0.5)
    per = LANES // head_dim
    rows = group * SIDE * COLS
    own = width // full.shape[0]

    @pl.when(pl.program_id(0) == 0)
    def _():
        copies = fetch(ids_ref, (one_ref, two_ref), full, sems)
        for copy in copies:
            copy.start()
        for copy in copies:
            copy.wait()
        vec[...] = vector_rows(full, 3 * own)

    ones = stacked(jnp.ones((KEYS, LANES), BF16), head_masks(head_dim))
    inputs = padded_rows(img_ref[...])
    hat, _ = moments(inputs)
    normed = (hat * vec[0:1] + vec[1:2]).astype(BF16)
    trip[rows:, :] = jnp.zeros((COLS, 3 * width), BF16)
    for c, extra in enumerate((vec[2:3], None, vec[3:4])):
        part = dot(normed, block_rows(full, c * own, own))
        if extra is not None:
            part = part + extra
        part = part.astype(BF16)
        trip[0:rows, c * width : (c + 1) * width] = part
        triple_ref[:, :, c * width : (c + 1) * width] = part.reshape(group, SIDE * COLS, width)
    masks = head_masks(head_dim)

    def pair(p, carry):
        start = pl.multiple_of(p * PAIR, COLS)
        for g in range(width // LANES):
            q = trip[pl.ds(start, PAIR), g * LANES : (g + 1) * LANES]
            k = trip[pl.ds(start, KEYS), width + g * LANES : width + (g + 1) * LANES]
            v = trip[pl.ds(start, KEYS), 2 * width + g * LANES : 2 * width + (g + 1) * LANES]
            scores = dot_nt(stacked(q, masks), k) * scale + bias_ref[g]
            top = jnp.max(scores, -1, keepdims=True)
            raised = jnp.exp(scores - top).astype(BF16)
            raised_ref[p, g] = raised
            both = dot(side_by_side(raised, per), jnp.concatenate([stacked(v, masks), ones], 1))
            inverse = 1.0 / both[:, LANES:]
            inverse_ref[p, :, g * LANES : (g + 1) * LANES] = inverse
            mixed = (both[:, :LANES] * inverse).astype(BF16)
            mixed_ref[p, :, g * LANES : (g + 1) * LANES] = mixed
        return carry

    lax.fori_loop(0, 2 * group, pair, 0, unroll=UNROLL)


def mlp_kernel(
    ids_ref, counts_ref, img_ref, cot_ref, mixed_ref, inverse_ref, one_ref, two_ref,
    out_ref, gres_ref, gmix_ref, keep_ref, send_ref,
    full, vec, acc1, acc2, accp, accv, accb, turned, sems,
):
    step = pl.program_id(0)
    group = img_ref.shape[0]
    width = img_ref.shape[-1]
    rows = group * SIDE * COLS
    chunks = acc1.shape[0]
    owners = full.shape[0]
    own = width // owners
    span = chunks * own
    at_one, at_proj, at_vec = span, 2 * span, 2 * span + own

    @pl.when(step == 0)
    def _():
        copies = fetch(ids_ref, (one_ref, two_ref), full, sems)
        for copy in copies:
            copy.start()
        for ref in (acc1, acc2, accp, accv, accb):
            ref[...] = jnp.zeros_like(ref)
        for copy in copies:
            copy.wait()
        vec[...] = vector_rows(full, at_vec)

    row = lax.broadcasted_iota(jnp.int32, (rows, 1), 0)
    image = row // (SIDE * COLS)
    live = ((step * group + image) < counts_ref[0]) & (row % COLS < SIDE)
    mixed = mixed_ref[...].reshape(rows, width)
    w_proj = block_rows(full, at_proj, own)
    residual = padded_rows(img_ref[...]) + dot(mixed, w_proj) + vec[0:1]
    hat, scale = moments(residual)
    gain = vec[1:2]
    normed = (hat * gain + vec[2:3]).astype(BF16)
    normed_t = normed.T
    grad_out = jnp.where(live, padded_rows(cot_ref[...]), 0.0)
    grad_low = grad_out.astype(BF16)
    grad_low_t = grad_low.T
    total, back = None, None
    for c in range(chunks):
        w1 = block_rows(full, at_one + c * own, own)
        half = owners // chunks
        w2 = full[c * half : (c + 1) * half, :span, :].reshape(width, width)
        hidden = dot(normed, w1) + vec[4 + c : 5 + c]
        below = 0.5 + 0.5 * lax.erf(hidden * (0.5**0.5))
        act = (hidden * below).astype(BF16)
        slope = below + hidden * (0.3989422804014327 * jnp.exp(-0.5 * hidden * hidden))
        after = dot(act, w2)
        total = after if total is None else total + after
        grad_hidden = (slope * dot_nt(grad_low, w2)).astype(BF16)
        before = dot_nt(grad_hidden, w1)
        back = before if back is None else back + before
        acc1[c] += dot(normed_t, grad_hidden)
        acc2[c] += dot(grad_low_t, act)
        accb[c : c + 1] += jnp.sum(grad_hidden.astype(F32), 0, keepdims=True)
    result = jnp.where(live, residual + total + vec[3:4], 0.0)
    out_ref[...] = unpadded(result, group).astype(BF16)
    grad_res = grad_out + norm_backward(back, hat, scale, gain)
    grad_res_low = grad_res.astype(BF16)
    gres_ref[...] = grad_res_low.reshape(group, SIDE * COLS, width)
    grad_mixed = dot_nt(grad_res_low, w_proj) * inverse_ref[...].reshape(rows, width)
    gmix_ref[...] = grad_mixed.astype(BF16).reshape(group, SIDE * COLS, width)
    accp[...] += dot(mixed.T, grad_res_low)
    accv[0:1] += jnp.sum(grad_res_low.astype(F32), 0, keepdims=True)
    accv[1:2] += jnp.sum(back * hat, 0, keepdims=True)
    accv[2:3] += jnp.sum(back, 0, keepdims=True)
    accv[3:4] += jnp.sum(grad_low.astype(F32), 0, keepdims=True)

    @pl.when(step == pl.num_programs(0) - 1)
    def _():
        for c in range(chunks):
            turned[c * width : (c + 1) * width] = acc2[c].astype(BF16).T
        sums = jnp.concatenate([accv[0:4], accb[0:4], jnp.zeros((8, width), F32)], 0).astype(BF16)
        half = owners // 2
        for number, ref in enumerate((keep_ref, send_ref)):

            def place(j, carry, ref=ref, number=number):
                owner = ids_ref[number * half + j]
                ref[j, 0:span] = turned[pl.ds(pl.multiple_of(owner * span, span), span)]
                mine = pl.ds(pl.multiple_of(owner * own, own), own)
                for c in range(chunks):
                    ref[j, at_one + c * own : at_one + (c + 1) * own] = acc1[c, mine].astype(BF16)
                ref[j, at_proj : at_proj + own] = accp[mine].astype(BF16)
                ref[j, at_vec : at_vec + VEC_ROWS] = sums
                return carry

            lax.fori_loop(0, half, place, 0)


def backward_kernel(
    heads, first, last, ids_ref, img_ref, gres_ref, gmix_ref, mixed_ref, triple_ref, raised_ref,
    one_ref, two_ref, choice_ref, *refs
):
    trip, gtrip, full, vec, sems = refs[-5:]
    step = pl.program_id(0)
    group = img_ref.shape[0]
    width = img_ref.shape[-1]
    head_dim = width // heads
    scale = head_dim ** (-0.5)
    per = LANES // head_dim
    rows = group * SIDE * COLS
    own = width // full.shape[0]
    carried = () if first else refs[1:4]
    outs = refs[0 if first else 4 : -5]
    gin_ref = outs[0]
    if last:
        keep_ref, send_ref, accw, accv, accb = outs[1:]
    else:
        accw, accv, accb = outs[1:]
    copies = fetch(ids_ref, (one_ref, two_ref), full, sems)

    @pl.when(step == 0)
    def _():
        for copy in copies:
            copy.start()
        if carried:
            accw[...] = carried[0][...]
            accv[...] = carried[1][...]
            accb[...] = carried[2][...]
        else:
            accw[...] = jnp.zeros_like(accw)
            accv[...] = jnp.zeros_like(accv)
            accb[...] = jnp.zeros_like(accb)

    trip[0:rows, :] = triple_ref[...].reshape(rows, 3 * width)
    trip[rows:, :] = jnp.zeros((COLS, 3 * width), BF16)
    masks = head_masks(head_dim)
    ones = jnp.ones((KEYS, LANES), BF16)

    def pair(p, carry):
        start = pl.multiple_of(p * PAIR, COLS)
        for g in range(width // LANES):
            lo, hi = g * LANES, (g + 1) * LANES
            q = trip[pl.ds(start, PAIR), lo:hi]
            k = trip[pl.ds(start, KEYS), width + lo : width + hi]
            v = trip[pl.ds(start, KEYS), 2 * width + lo : 2 * width + hi]
            raised = raised_ref[p, g]
            grad_mixed = gmix_ref[p, :, lo:hi]
            inner = -(grad_mixed.astype(F32) * mixed_ref[p, :, lo:hi].astype(F32))
            left = jnp.concatenate(
                [stacked(grad_mixed, masks), stacked(inner.astype(BF16), masks)], 1
            )
            grad_probs = dot_nt(left, jnp.concatenate([v, ones], 1))
            grad_scores = (raised.astype(F32) * grad_probs).astype(BF16)
            accb[g] += grad_scores.astype(F32)
            wide = side_by_side(grad_scores, per)
            grad_q = dot(wide, stacked(k, masks)) * scale
            grad_k = own_blocks(dot(q.T, wide), per) * scale
            grad_v = own_blocks(dot(grad_mixed.T, side_by_side(raised, per)), per)
            gtrip[pl.ds(start, PAIR), lo:hi] = grad_q.astype(BF16)
            gtrip[pl.ds(start, PAIR), width + lo : width + hi] = grad_k.astype(BF16).T[:PAIR]
            gtrip[pl.ds(start, PAIR), 2 * width + lo : 2 * width + hi] = grad_v.astype(BF16).T[:PAIR]
        return carry

    lax.fori_loop(0, 2 * group, pair, 0, unroll=UNROLL)

    @pl.when(step == 0)
    def _():
        for copy in copies:
            copy.wait()
        vec[...] = vector_rows(full, 3 * own)

    hat, norm_scale = moments(padded_rows(img_ref[...]))
    gain = vec[0:1]
    normed_t = (hat * gain + vec[1:2]).astype(BF16).T
    back = None
    for c in range(3):
        part = gtrip[:, c * width : (c + 1) * width]
        accw[c] += dot(normed_t, part)
        accv[2 + c : 3 + c] += jnp.sum(part.astype(F32), 0, keepdims=True)
        before = dot_nt(part, block_rows(full, c * own, own))
        back = before if back is None else back + before
    accv[0:1] += jnp.sum(back * hat, 0, keepdims=True)
    accv[1:2] += jnp.sum(back, 0, keepdims=True)
    grad_in = gres_ref[...].reshape(rows, width) + norm_backward(back, hat, norm_scale, gain)
    gin_ref[...] = unpadded(grad_in, group).astype(BF16)

    if last:

        @pl.when(step == pl.num_programs(0) - 1)
        def _():
            query = lax.broadcasted_iota(jnp.int32, (PAIR, PAIR), 0)
            other = lax.broadcasted_iota(jnp.int32, (PAIR, PAIR), 1)
            turn = jnp.where(query + other == PAIR - 1, 1.0, 0.0).astype(BF16)
            sums = []
            for h in range(heads):
                tile = accb[h // per, h % per * PAIR : (h % per + 1) * PAIR]
                high = tile.astype(BF16)
                low = (tile - high.astype(F32)).astype(BF16)
                back_to_front = dot(turn, jnp.concatenate([high, low], 1))
                back_to_front = back_to_front[:, :KEYS] + back_to_front[:, KEYS:]
                wide = jnp.concatenate([back_to_front, jnp.zeros_like(back_to_front)], 1)
                skewed = pltpu.roll(wide, 0, 1, stride=1, stride_axis=0)
                sums.append(jnp.sum(skewed, 0, keepdims=True))
            sums = pltpu.roll(jnp.concatenate(sums, 0), 2 * KEYS - PAIR + 1, 1)
            high = sums.astype(BF16)
            low = (sums - high.astype(F32)).astype(BF16)
            table = dot(high, choice_ref[...]) + dot(low, choice_ref[...])
            pieces = width // LANES
            vectors = jnp.concatenate(
                [
                    accv[v : v + 1, i * LANES : (i + 1) * LANES]
                    for v in (0, 1, 2, 4)
                    for i in range(pieces)
                ],
                0,
            )
            rest = width - table.shape[1] - LANES
            tile = jnp.concatenate([table, vectors, jnp.zeros((VEC_ROWS, rest), F32)], 1).astype(BF16)
            half = full.shape[0] // 2
            for number, ref in enumerate((keep_ref, send_ref)):

                def place(j, carry, ref=ref, number=number):
                    owner = ids_ref[number * half + j]
                    mine = pl.ds(pl.multiple_of(owner * own, own), own)
                    for c in range(3):
                        ref[j, c * own : (c + 1) * own] = accw[c, mine].astype(BF16)
                    ref[j, 3 * own : 3 * own + VEC_ROWS] = tile
                    return carry

                lax.fori_loop(0, half, place, 0)


def bias_kernel(table_ref, seen_ref, bias_ref):
    heads = table_ref.shape[0]
    per = bias_ref.shape[1] // PAIR
    for h in range(heads):
        row = jnp.broadcast_to(table_ref[h : h + 1], (PAIR, table_ref.shape[1]))
        skewed = pltpu.roll(row, 0, 1, stride=1, stride_axis=0)
        at = h % per * PAIR
        bias_ref[h // per, at : at + PAIR] = jnp.where(seen_ref[...] > 0, skewed[:, :KEYS], NEG)


def whole(shape):
    return pl.BlockSpec(shape, lambda *_: (0,) * len(shape))


def params(mib):
    return pltpu.CompilerParams(
        dimension_semantics=("arbitrary",), vmem_limit_bytes=mib * MIB
    )


def image_group(slots):
    return 2 if slots % 2 == 0 else 1


def split_steps(steps, shares):
    if steps < 2 * len(shares):
        return [steps]
    sizes = [max(1, int(steps * share + 0.5)) for share in shares[:-1]]
    return sizes + [steps - sum(sizes)]


ANY = pl.BlockSpec(memory_space=pl.ANY)
SMEM = pl.BlockSpec(memory_space=pltpu.SMEM)


def weight_scratch(pieces):
    owners = 2 * pieces[0].shape[0]
    shape = (owners,) + pieces[0].shape[1:]
    return [
        pltpu.VMEM(shape, BF16),
        pltpu.VMEM((VEC_ROWS, shape[-1]), F32),
    ], pltpu.SemaphoreType.DMA((owners,))


def attention_forward(ids, images, pieces, bias, heads, first, steps, group, carried):
    slots, width = images.shape[0], images.shape[-1]
    tokens = SIDE * COLS
    groups, stack = bias.shape[:2]
    block = lambda i: (first + i, 0, 0)
    block4 = lambda i: (first + i, 0, 0, 0)
    full, sems = weight_scratch(pieces)
    return pl.pallas_call(
        partial(forward_kernel, heads, len(carried)),
        grid=(steps,),
        in_specs=[
            SMEM,
            pl.BlockSpec((group, SIDE, SIDE, width), block4),
            ANY,
            ANY,
            whole(bias.shape),
        ]
        + [ANY] * len(carried),
        out_specs=[
            pl.BlockSpec((group, tokens, 3 * width), block),
            pl.BlockSpec((2 * group, groups, stack, KEYS), block4),
            pl.BlockSpec((2 * group, PAIR, width), block),
            pl.BlockSpec((2 * group, PAIR, width), block),
        ],
        out_shape=[
            jax.ShapeDtypeStruct((slots, tokens, 3 * width), BF16),
            jax.ShapeDtypeStruct((2 * slots, groups, stack, KEYS), BF16),
            jax.ShapeDtypeStruct((2 * slots, PAIR, width), BF16),
            jax.ShapeDtypeStruct((2 * slots, PAIR, width), F32),
        ],
        scratch_shapes=[pltpu.VMEM((group * tokens + COLS, 3 * width), BF16), *full, sems],
        input_output_aliases={5 + i: i for i in range(len(carried))},
        compiler_params=params(56),
        cost_estimate=pl.CostEstimate(
            flops=steps * group * tokens * width * width * 40,
            bytes_accessed=steps * group * 2 * MIB,
            transcendentals=0,
        ),
        name="attention_forward",
    )(ids, images, *pieces, bias, *carried)


def feed_forward(ids, counts, images, cotangent, mixed, inverse, pieces, chunks):
    slots, width = images.shape[0], images.shape[-1]
    group = next(g for g in (4, 2, 1) if slots % g == 0)
    tokens = SIDE * COLS
    image_spec = pl.BlockSpec((group, SIDE, SIDE, width), lambda i: (i, 0, 0, 0))
    row_spec = pl.BlockSpec((group, tokens, width), lambda i: (i, 0, 0))
    half = pieces[0].shape
    outs = [
        (images.shape, BF16, image_spec),
        ((slots, tokens, width), BF16, row_spec),
        ((slots, tokens, width), BF16, row_spec),
        (half, BF16, whole(half)),
        (half, BF16, whole(half)),
    ]
    full, sems = weight_scratch(pieces)
    return pl.pallas_call(
        mlp_kernel,
        grid=(slots // group,),
        in_specs=[SMEM, SMEM, image_spec, image_spec, row_spec, row_spec, ANY, ANY],
        out_specs=[o[2] for o in outs],
        out_shape=[jax.ShapeDtypeStruct(o[0], o[1]) for o in outs],
        scratch_shapes=[
            *full,
            pltpu.VMEM((chunks, width, width), F32),
            pltpu.VMEM((chunks, width, width), F32),
            pltpu.VMEM((width, width), F32),
            pltpu.VMEM((8, width), F32),
            pltpu.VMEM((8, width), F32),
            pltpu.VMEM((chunks * width, width), BF16),
            sems,
        ],
        compiler_params=params(62),
        cost_estimate=pl.CostEstimate(
            flops=slots * tokens * width * width * (3 + chunks * 6) * 4,
            bytes_accessed=32 * MIB,
            transcendentals=0,
        ),
        name="feed_forward",
    )(ids, counts, images, cotangent, mixed, inverse, *pieces)


def attention_backward(
    ids, images, gres, gmix, mixed, triple, probs, pieces, choice, heads, first, steps, group,
    carried, last,
):
    slots, width = images.shape[0], images.shape[-1]
    tokens = SIDE * COLS
    groups, stack = probs.shape[1:3]
    block = lambda i: (first + i, 0, 0)
    block4 = lambda i: (first + i, 0, 0, 0)
    image_spec = pl.BlockSpec((group, SIDE, SIDE, width), block4)
    sums = [(3, width, width), (8, width), (groups, stack, KEYS)]
    half = pieces[0].shape
    outs = [(s, F32) for s in sums] if not last else [(half, BF16), (half, BF16)]
    full, sems = weight_scratch(pieces)
    return pl.pallas_call(
        partial(backward_kernel, heads, not carried, last),
        grid=(steps,),
        in_specs=[
            SMEM,
            image_spec,
            pl.BlockSpec((group, tokens, width), block),
            pl.BlockSpec((2 * group, PAIR, width), block),
            pl.BlockSpec((2 * group, PAIR, width), block),
            pl.BlockSpec((group, tokens, 3 * width), block),
            pl.BlockSpec((2 * group, groups, stack, KEYS), block4),
            ANY,
            ANY,
            whole(choice.shape),
        ]
        + ([ANY] + [whole(s) for s in sums] if carried else []),
        out_specs=[image_spec] + [whole(s) for s, _ in outs],
        out_shape=[jax.ShapeDtypeStruct(images.shape, BF16)]
        + [jax.ShapeDtypeStruct(s, k) for s, k in outs],
        scratch_shapes=([pltpu.VMEM(s, F32) for s in sums] if last else [])
        + [
            pltpu.VMEM((group * tokens + COLS, 3 * width), BF16),
            pltpu.VMEM((group * tokens, 3 * width), BF16),
            *full,
            sems,
        ],
        input_output_aliases={10: 0} if carried else {},
        compiler_params=params(62),
        cost_estimate=pl.CostEstimate(
            flops=steps * group * tokens * width * width * 90,
            bytes_accessed=steps * group * 4 * MIB,
            transcendentals=0,
        ),
        name="attention_backward",
    )(ids, images, gres, gmix, mixed, triple, probs, *pieces, choice, *carried)


def expand_bias(table, seen, heads, per):
    return pl.pallas_call(
        bias_kernel,
        out_shape=jax.ShapeDtypeStruct((heads // per, per * PAIR, KEYS), F32),
        name="expand_bias",
    )(table, seen)


def flip(values, bits, devices):
    return lax.ppermute(values, "dev", [(i, i ^ bits) for i in range(devices)])


def exchange_groups(devices):
    bits = [1 << i for i in range(devices.bit_length() - 1)]
    return [bits[:1]] + [bits[i : i + 2] for i in range(1, len(bits), 2)]


def mixes(group):
    found = [0]
    for bit in group:
        found = found + [f ^ bit for f in found]
    return found


def block_order(devices):
    order = [0]
    for group in exchange_groups(devices)[:0:-1]:
        order = [m ^ o for m in mixes(group) for o in order]
    return order + [exchange_groups(devices)[0][0] ^ o for o in order]


def gather_parts(held, group, devices):
    return [held] + [flip(held, m, devices) for m in mixes(group)[1:]]


def gather_group(held, group, devices):
    return jnp.concatenate(gather_parts(held, group, devices))


def share_parts(held, group, devices):
    parts = jnp.split(held, 2 ** len(group))
    return parts[:1] + [flip(part, m, devices) for part, m in zip(parts[1:], mixes(group)[1:])]


def add_parts(parts):
    sums = [part.astype(F32) for part in parts]
    while len(sums) > 1:
        sums = [a + b for a, b in zip(sums[::2], sums[1::2])]
    return sums[0]


def tie(first, second):
    return lax.optimization_barrier((first, second))


def offsets():
    picks = np.full((2 * KEYS,), -1, np.int64)
    area = WINDOW * WINDOW
    for i in range(area):
        for j in range(area):
            place = (j // WINDOW - i // WINDOW) * COLS + j % WINDOW - i % WINDOW
            picks[place % (2 * KEYS)] = i * area + j
    return picks


def seen_keys():
    place = np.arange(KEYS)
    row, col = place // COLS, place % COLS
    side = np.where(col < SIDE, col // WINDOW, 2)
    ok = (row < WINDOW) & (side < 2)
    seen = (side[:PAIR, None] == side[None]) & ok[:PAIR, None] & ok[None]
    return seen.astype(np.float32)


def owner_lanes(vectors, me, devices):
    share = vectors.shape[-1]
    lane = lax.broadcasted_iota(jnp.int32, (1, share * devices), 1)
    return jnp.where(lane // share == me, jnp.tile(vectors, (1, devices)), 0)


def regroup(pieces, order, fields, me, devices, owners):
    by_number = np.argsort(np.array(order))
    blocks = jnp.concatenate(pieces)
    blocks = jnp.take(blocks, jnp.asarray(by_number)[jnp.arange(devices) ^ me], axis=0)
    out, at = [], 0
    for rows in fields:
        out.append(blocks[:, at : at + rows].reshape(owners, -1, blocks.shape[-1]))
        at += rows
    vectors = blocks[:, at:].reshape(owners, devices // owners, VEC_ROWS, -1)
    out.append(jnp.sum(vectors.astype(F32), 1).astype(BF16))
    return jnp.split(jnp.concatenate(out, 1), 2)


def ungroup(pieces, order, fields, me, devices, owners):
    blocks = jnp.concatenate(pieces)
    many = devices // owners
    out, at = [], 0
    for rows in fields:
        rows = rows * many
        out.append(blocks[:, at : at + rows].reshape(devices, rows // many, -1))
        at += rows
    out.append(jnp.repeat(blocks[:, at:], many, axis=0))
    blocks = jnp.take(jnp.concatenate(out, 1), jnp.asarray(np.array(order)) ^ me, axis=0)
    return jnp.split(blocks, 2)


def shards(
    devices,
    images,
    cotangent,
    image_counts,
    rel_index,
    ln1_gain,
    ln1_shift,
    w_qkv,
    q_bias,
    v_bias,
    w_proj,
    b_proj,
    ln2_gain,
    ln2_shift,
    w_fc1,
    b_fc1,
    w_fc2,
    b_fc2,
    bias_table,
):
    me = lax.axis_index("dev")
    slots, width = images.shape[0], images.shape[3]
    table_rows, heads = bias_table.shape
    own = ln1_gain.shape[0]
    span = b_fc1.shape[0]
    chunks = span // own
    per = LANES // (width // heads)
    groups = exchange_groups(devices)
    order = block_order(devices)
    aligned = own % COLS == 0
    owners = devices if aligned else width // COLS
    attn_fields = [own] * 3
    mlp_fields = [span] + [own] * (chunks + 1)
    if aligned:
        ids = jnp.asarray(np.array(order, np.int32)) ^ me
    else:
        ids = jnp.arange(owners, dtype=jnp.int32)

    attn_vec = owner_lanes(jnp.stack([ln1_gain, ln1_shift, q_bias, v_bias]), me, devices)
    attn_block = jnp.concatenate(
        [w_qkv[:, c * width : (c + 1) * width] for c in range(3)]
        + [attn_vec, jnp.zeros((VEC_ROWS - 4, width), BF16)]
    )
    mlp_vec = owner_lanes(jnp.stack([b_proj, ln2_gain, ln2_shift, b_fc2]), me, devices)
    hidden_vec = owner_lanes(b_fc1[None], me, devices).reshape(chunks, width)
    mlp_block = jnp.concatenate(
        [w_fc2]
        + [w_fc1[:, c * width : (c + 1) * width] for c in range(chunks)]
        + [w_proj, mlp_vec, hidden_vec, jnp.zeros((VEC_ROWS - 4 - chunks, width), BF16)]
    )
    far = groups[:0:-1]

    picks = offsets()
    rows_of = rel_index.reshape(-1)[np.maximum(picks, 0)]
    rows_of = jnp.where(jnp.asarray(picks) >= 0, rows_of, -1)
    choice = (rows_of[:, None] == jnp.arange(2 * KEYS, dtype=jnp.int32)).astype(BF16)
    table = jnp.pad(bias_table, ((0, 2 * KEYS - table_rows), (0, 0))).T
    high = table.astype(BF16)
    mid = (table - high.astype(F32)).astype(BF16)
    low = (table - high.astype(F32) - mid.astype(F32)).astype(BF16)
    by_offset = dot_nt(jnp.concatenate([high, mid, low]), choice)
    by_offset = by_offset[:heads] + by_offset[heads : 2 * heads] + by_offset[2 * heads :]
    bias = expand_bias(by_offset, jnp.asarray(seen_keys()), heads, per)

    held = jnp.concatenate([attn_block, mlp_block])[None]
    for bits in far[:-1]:
        held = gather_group(held, bits, devices)
    attn_held, mlp_held = held[:, : attn_block.shape[0]], held[:, attn_block.shape[0] :]
    attn_held = gather_group(attn_held, far[-1], devices)
    attn_held, mlp_held = tie(attn_held, mlp_held)
    bias, attn_held = tie(bias, attn_held)
    attn_pieces = (attn_held, flip(attn_held, groups[0][0], devices))
    if not aligned:
        attn_pieces = regroup(attn_pieces, order, attn_fields, me, devices, owners)

    group = image_group(slots)
    sizes = split_steps(slots // group, (5 / 6, 1 / 6))
    mlp_parts = gather_parts(mlp_held, far[-1], devices)
    carried, first = (), 0
    for steps in sizes:
        if carried:
            carried, mlp_parts = tie(carried, mlp_parts)
        carried = attention_forward(
            ids, images, attn_pieces, bias, heads, first, steps, group, carried
        )
        first += steps
    mlp_held = jnp.concatenate(mlp_parts)
    triple, raised, mixed, inverse = carried
    mlp_pieces = (mlp_held, flip(mlp_held, groups[0][0], devices))
    if not aligned:
        mlp_pieces = regroup(mlp_pieces, order, mlp_fields, me, devices, owners)
    output, gres, gmix, *mlp_sums = feed_forward(
        ids,
        image_counts,
        images,
        cotangent,
        mixed.reshape(slots, SIDE * COLS, width),
        inverse.reshape(slots, SIDE * COLS, width),
        mlp_pieces,
        chunks,
    )

    if not aligned:
        mlp_sums = ungroup(mlp_sums, order, mlp_fields, me, devices, owners)
    gmix = gmix.reshape(2 * slots, PAIR, width)
    sizes = split_steps(slots // group, (1 / 6, 1 / 2, 1 / 3))
    left = groups[1:]
    parts = [mlp_sums[0], flip(mlp_sums[1], groups[0][0], devices)]
    carried, first = (), 0
    for call, steps in enumerate(sizes):
        if carried:
            carried, parts = tie(carried, parts)
            if left:
                parts = share_parts(add_parts(parts).astype(BF16), left[0], devices)
                left = left[1:]
        carried = attention_backward(
            ids, images, gres, gmix, mixed, triple, raised, attn_pieces, choice, heads, first,
            steps, group, tuple(carried), call == len(sizes) - 1,
        )
        first += steps
    for bits in left:
        parts = share_parts(add_parts(parts).astype(BF16), bits, devices)
    if len(sizes) > 1:
        carried, parts = tie(carried, parts)
    mlp_mine = add_parts(parts).reshape(-1, width)

    grad_input, *attn_sums = carried
    if not aligned:
        attn_sums = ungroup(attn_sums, order, attn_fields, me, devices, owners)
    mine = add_parts([attn_sums[0], flip(attn_sums[1], groups[0][0], devices)])
    for bits in groups[1:]:
        mine = add_parts(share_parts(mine.astype(BF16), bits, devices))
    mine = mine.reshape(-1, width)

    grad_fc2 = mlp_mine[:span]
    at = span
    grad_fc1 = jnp.concatenate(
        [mlp_mine[at + c * own : at + (c + 1) * own] for c in range(chunks)], 1
    )
    at += chunks * own
    grad_proj = mlp_mine[at : at + own]
    at += own
    vectors = lax.dynamic_slice_in_dim(mlp_mine[at : at + 4], me * own, own, 1)
    grad_proj_bias, grad_gain_two, grad_shift_two, grad_fc2_bias = vectors
    grad_fc1_bias = lax.dynamic_slice_in_dim(
        mlp_mine[at + 4 : at + 4 + chunks].reshape(-1), me * span, span, 0
    )

    grad_qkv = jnp.concatenate([mine[c * own : (c + 1) * own] for c in range(3)], 1)
    tile = mine[3 * own :]
    table_total = tile[:heads, :table_rows].T
    vectors = tile[:, 2 * KEYS : 2 * KEYS + LANES].reshape(4, width)
    vectors = lax.dynamic_slice_in_dim(vectors, me * own, own, 1)
    grad_gain_one, grad_shift_one, grad_query_bias, grad_value_bias = vectors
    return (
        output,
        grad_input,
        grad_gain_one,
        grad_shift_one,
        grad_qkv,
        grad_query_bias,
        grad_value_bias,
        grad_proj,
        grad_proj_bias,
        grad_gain_two,
        grad_shift_two,
        grad_fc1,
        grad_fc1_bias,
        grad_fc2,
        grad_fc2_bias,
        table_total,
    )


def solution(mesh):
    rows = P("dev", None)
    image = P("dev", None, None, None)
    flat = P("dev")
    in_specs = (
        image, image, flat, P(), flat, flat, rows, flat, flat, rows, flat,
        flat, flat, rows, flat, rows, flat, P(),
    )
    out_specs = (
        image, image, flat, flat, rows, flat, flat, rows, flat,
        flat, flat, rows, flat, rows, flat, P(),
    )
    body = partial(shards, mesh.shape["dev"])
    return jax.shard_map(body, mesh=mesh, in_specs=in_specs, out_specs=out_specs, check_vma=False)
```

```python
from functools import partial

import jax
import jax.numpy as jnp
import numpy as np
from jax import lax
from jax.experimental import pallas as pl
from jax.experimental.pallas import tpu as pltpu
from jax.sharding import PartitionSpec as P

WINDOW = 7
SIDE = 14
COLS = 16
PAIR = WINDOW * COLS
KEYS = 128
LANES = 128
EPSILON = 1e-05
HIGHEST = lax.Precision.HIGHEST
MIB = 2**20
NEG = -1e30
VEC_ROWS = 16
UNROLL = 4
F32 = jnp.float32
BF16 = jnp.bfloat16


def dot(left, right):
    return lax.dot_general(left, right, (((1,), (0,)), ((), ())), preferred_element_type=F32)


def dot_nt(left, right):
    return lax.dot_general(left, right, (((1,), (1,)), ((), ())), preferred_element_type=F32)


def dot_tn(left, right):
    return lax.dot_general(left, right, (((0,), (0,)), ((), ())), preferred_element_type=F32)


def padded_rows(block):
    wide = block.astype(F32)
    wide = jnp.pad(wide, ((0, 0), (0, 0), (0, COLS - SIDE), (0, 0)))
    return wide.reshape(-1, block.shape[-1])


def unpadded(rows, images):
    return rows.reshape(images, SIDE, COLS, rows.shape[-1])[:, :, :SIDE, :]


def moments(values):
    center = values - jnp.mean(values, -1, keepdims=True)
    spread = jnp.mean(center * center, -1, keepdims=True)
    scale = lax.rsqrt(spread + EPSILON)
    return center * scale, scale


def norm_backward(grad, hat, scale, gain):
    inner = grad * gain
    mean_one = jnp.mean(inner, -1, keepdims=True)
    mean_two = jnp.mean(inner * hat, -1, keepdims=True)
    return scale * (inner - mean_one - hat * mean_two)


def head_masks(head_dim):
    lane = lax.broadcasted_iota(jnp.int32, (1, LANES), 1) // head_dim
    return [lane == h for h in range(LANES // head_dim)]


def stacked(block, masks):
    zero = jnp.zeros_like(block)
    return jnp.concatenate([jnp.where(m, block, zero) for m in masks], 0)


def side_by_side(tall, parts):
    rows = tall.shape[0] // parts
    return jnp.concatenate([tall[i * rows : (i + 1) * rows] for i in range(parts)], 1)


def fetch(ids_ref, pieces, full, sems):
    copies = []
    for number, piece in enumerate(pieces):
        count = piece.shape[0]
        for j in range(count):
            at = number * count + j
            copies.append(
                pltpu.make_async_copy(piece.at[j], full.at[ids_ref[at]], sems.at[at])
            )
    return copies


def block_rows(full, start, rows):
    part = full[:, start : start + rows, :]
    return part.reshape(-1, part.shape[-1])


def vector_rows(full, start):
    return jnp.sum(full[:, start : start + VEC_ROWS, :].astype(F32), 0)


def head_pairs(heads):
    return [slice(h, min(h + 2, heads)) for h in range(0, heads, 2)]


def own_blocks(products, parts):
    rows, lanes = products.shape[0] // parts, products.shape[1] // parts
    return jnp.concatenate(
        [products[i * rows : (i + 1) * rows, i * lanes : (i + 1) * lanes] for i in range(parts)], 0
    )


def forward_kernel(heads, carried, ids_ref, img_ref, one_ref, two_ref, bias_ref, *refs):
    triple_ref, raised_ref, mixed_ref, inverse_ref, trip, full, vec, sems = refs[carried:]
    group = img_ref.shape[0]
    width = img_ref.shape[-1]
    head_dim = width // heads
    scale = head_dim ** (-0.5)
    per = LANES // head_dim
    rows = group * SIDE * COLS
    own = width // full.shape[0]

    @pl.when(pl.program_id(0) == 0)
    def _():
        copies = fetch(ids_ref, (one_ref, two_ref), full, sems)
        for copy in copies:
            copy.start()
        for copy in copies:
            copy.wait()
        vec[...] = vector_rows(full, 3 * own)

    ones = stacked(jnp.ones((KEYS, LANES), BF16), head_masks(head_dim))
    inputs = padded_rows(img_ref[...])
    hat, _ = moments(inputs)
    normed = (hat * vec[0:1] + vec[1:2]).astype(BF16)
    trip[rows:, :] = jnp.zeros((COLS, 3 * width), BF16)
    for c, extra in enumerate((vec[2:3], None, vec[3:4])):
        part = dot(normed, block_rows(full, c * own, own))
        if extra is not None:
            part = part + extra
        part = part.astype(BF16)
        trip[0:rows, c * width : (c + 1) * width] = part
        triple_ref[:, :, c * width : (c + 1) * width] = part.reshape(group, SIDE * COLS, width)
    masks = head_masks(head_dim)

    def pair(p, carry):
        start = pl.multiple_of(p * PAIR, COLS)
        for g in range(width // LANES):
            q = trip[pl.ds(start, PAIR), g * LANES : (g + 1) * LANES]
            k = trip[pl.ds(start, KEYS), width + g * LANES : width + (g + 1) * LANES]
            v = trip[pl.ds(start, KEYS), 2 * width + g * LANES : 2 * width + (g + 1) * LANES]
            tiles = []
            for some in head_pairs(per):
                part = slice(some.start * PAIR, some.stop * PAIR)
                scores = dot_nt(stacked(q, masks[some]), k) * scale + bias_ref[g, part]
                top = jnp.max(scores, -1, keepdims=True)
                tiles.append(jnp.exp(scores - top).astype(BF16))
                raised_ref[p, g, part] = tiles[-1]
            raised = jnp.concatenate(tiles, 0)
            both = dot(side_by_side(raised, per), jnp.concatenate([stacked(v, masks), ones], 1))
            inverse = 1.0 / both[:, LANES:]
            inverse_ref[p, :, g * LANES : (g + 1) * LANES] = inverse
            mixed = (both[:, :LANES] * inverse).astype(BF16)
            mixed_ref[p, :, g * LANES : (g + 1) * LANES] = mixed
        return carry

    lax.fori_loop(0, 2 * group, pair, 0, unroll=UNROLL)


def mlp_kernel(
    ids_ref, counts_ref, img_ref, cot_ref, mixed_ref, inverse_ref, one_ref, two_ref,
    out_ref, gres_ref, gmix_ref, keep_ref, send_ref,
    full, vec, acc1, acc2, accp, accv, accb, turned, sems,
):
    step = pl.program_id(0)
    group = img_ref.shape[0]
    width = img_ref.shape[-1]
    rows = group * SIDE * COLS
    chunks = acc1.shape[0]
    owners = full.shape[0]
    own = width // owners
    span = chunks * own
    at_one, at_proj, at_vec = span, 2 * span, 2 * span + own

    @pl.when(step == 0)
    def _():
        copies = fetch(ids_ref, (one_ref, two_ref), full, sems)
        for copy in copies:
            copy.start()
        for ref in (acc1, acc2, accp, accv, accb):
            ref[...] = jnp.zeros_like(ref)
        for copy in copies:
            copy.wait()
        vec[...] = vector_rows(full, at_vec)

    row = lax.broadcasted_iota(jnp.int32, (rows, 1), 0)
    image = row // (SIDE * COLS)
    live = ((step * group + image) < counts_ref[0]) & (row % COLS < SIDE)
    mixed = mixed_ref[...].reshape(rows, width)
    w_proj = block_rows(full, at_proj, own)
    residual = padded_rows(img_ref[...]) + dot(mixed, w_proj) + vec[0:1]
    hat, scale = moments(residual)
    gain = vec[1:2]
    normed = (hat * gain + vec[2:3]).astype(BF16)
    normed_t = normed.T
    grad_out = jnp.where(live, padded_rows(cot_ref[...]), 0.0)
    grad_low = grad_out.astype(BF16)
    grad_low_t = grad_low.T
    total, back = None, None
    for c in range(chunks):
        w1 = block_rows(full, at_one + c * own, own)
        half = owners // chunks
        w2 = full[c * half : (c + 1) * half, :span, :].reshape(width, width)
        hidden = dot(normed, w1) + vec[4 + c : 5 + c]
        below = 0.5 + 0.5 * lax.erf(hidden * (0.5**0.5))
        act = (hidden * below).astype(BF16)
        slope = below + hidden * (0.3989422804014327 * jnp.exp(-0.5 * hidden * hidden))
        after = dot(act, w2)
        total = after if total is None else total + after
        grad_hidden = (slope * dot_nt(grad_low, w2)).astype(BF16)
        before = dot_nt(grad_hidden, w1)
        back = before if back is None else back + before
        acc1[c] += dot(normed_t, grad_hidden)
        acc2[c] += dot(grad_low_t, act)
        accb[c : c + 1] += jnp.sum(grad_hidden.astype(F32), 0, keepdims=True)
    result = jnp.where(live, residual + total + vec[3:4], 0.0)
    out_ref[...] = unpadded(result, group).astype(BF16)
    grad_res = grad_out + norm_backward(back, hat, scale, gain)
    grad_res_low = grad_res.astype(BF16)
    gres_ref[...] = grad_res_low.reshape(group, SIDE * COLS, width)
    grad_mixed = dot_nt(grad_res_low, w_proj) * inverse_ref[...].reshape(rows, width)
    gmix_ref[...] = grad_mixed.astype(BF16).reshape(group, SIDE * COLS, width)
    accp[...] += dot(mixed.T, grad_res_low)
    accv[0:1] += jnp.sum(grad_res_low.astype(F32), 0, keepdims=True)
    accv[1:2] += jnp.sum(back * hat, 0, keepdims=True)
    accv[2:3] += jnp.sum(back, 0, keepdims=True)
    accv[3:4] += jnp.sum(grad_low.astype(F32), 0, keepdims=True)

    @pl.when(step == pl.num_programs(0) - 1)
    def _():
        for c in range(chunks):
            turned[c * width : (c + 1) * width] = acc2[c].astype(BF16).T
        sums = jnp.concatenate([accv[0:4], accb[0:4], jnp.zeros((8, width), F32)], 0).astype(BF16)
        half = owners // 2
        for number, ref in enumerate((keep_ref, send_ref)):

            def place(j, carry, ref=ref, number=number):
                owner = ids_ref[number * half + j]
                ref[j, 0:span] = turned[pl.ds(pl.multiple_of(owner * span, span), span)]
                mine = pl.ds(pl.multiple_of(owner * own, own), own)
                for c in range(chunks):
                    ref[j, at_one + c * own : at_one + (c + 1) * own] = acc1[c, mine].astype(BF16)
                ref[j, at_proj : at_proj + own] = accp[mine].astype(BF16)
                ref[j, at_vec : at_vec + VEC_ROWS] = sums
                return carry

            lax.fori_loop(0, half, place, 0)


def backward_kernel(
    heads, first, last, ids_ref, img_ref, gres_ref, gmix_ref, mixed_ref, triple_ref, raised_ref,
    one_ref, two_ref, choice_ref, *refs
):
    trip, gtrip, full, vec, sems = refs[-5:]
    step = pl.program_id(0)
    group = img_ref.shape[0]
    width = img_ref.shape[-1]
    head_dim = width // heads
    scale = head_dim ** (-0.5)
    per = LANES // head_dim
    rows = group * SIDE * COLS
    own = width // full.shape[0]
    carried = () if first else refs[1:4]
    outs = refs[0 if first else 4 : -5]
    gin_ref = outs[0]
    if last:
        keep_ref, send_ref, accw, accv, accb = outs[1:]
    else:
        accw, accv, accb = outs[1:]
    copies = fetch(ids_ref, (one_ref, two_ref), full, sems)

    @pl.when(step == 0)
    def _():
        for copy in copies:
            copy.start()
        if carried:
            accw[...] = carried[0][...]
            accv[...] = carried[1][...]
            accb[...] = carried[2][...]
        else:
            accw[...] = jnp.zeros_like(accw)
            accv[...] = jnp.zeros_like(accv)
            accb[...] = jnp.zeros_like(accb)

    trip[0:rows, :] = triple_ref[...].reshape(rows, 3 * width)
    trip[rows:, :] = jnp.zeros((COLS, 3 * width), BF16)
    masks = head_masks(head_dim)
    ones = jnp.ones((KEYS, LANES), BF16)

    def pair(p, carry):
        start = pl.multiple_of(p * PAIR, COLS)
        for g in range(width // LANES):
            lo, hi = g * LANES, (g + 1) * LANES
            q = trip[pl.ds(start, PAIR), lo:hi]
            k = trip[pl.ds(start, KEYS), width + lo : width + hi]
            v = trip[pl.ds(start, KEYS), 2 * width + lo : 2 * width + hi]
            raised = raised_ref[p, g]
            grad_mixed = gmix_ref[p, :, lo:hi]
            inner = -(grad_mixed.astype(F32) * mixed_ref[p, :, lo:hi].astype(F32))
            inner = inner.astype(BF16)
            right = jnp.concatenate([v, ones], 1)
            tiles = []
            for some in head_pairs(per):
                part = slice(some.start * PAIR, some.stop * PAIR)
                left = [stacked(grad_mixed, masks[some]), stacked(inner, masks[some])]
                grad_probs = dot_nt(jnp.concatenate(left, 1), right)
                tiles.append((raised_ref[p, g, part].astype(F32) * grad_probs).astype(BF16))
                accb[g, part] += tiles[-1].astype(F32)
            grad_scores = jnp.concatenate(tiles, 0)
            wide = side_by_side(grad_scores, per)
            grad_q = dot(wide, stacked(k, masks)) * scale
            grad_k = own_blocks(dot(q.T, wide), per) * scale
            grad_v = own_blocks(dot(grad_mixed.T, side_by_side(raised, per)), per)
            gtrip[pl.ds(start, PAIR), lo:hi] = grad_q.astype(BF16)
            gtrip[pl.ds(start, PAIR), width + lo : width + hi] = grad_k.astype(BF16).T[:PAIR]
            gtrip[pl.ds(start, PAIR), 2 * width + lo : 2 * width + hi] = grad_v.astype(BF16).T[:PAIR]
        return carry

    lax.fori_loop(0, 2 * group, pair, 0, unroll=UNROLL)

    @pl.when(step == 0)
    def _():
        for copy in copies:
            copy.wait()
        vec[...] = vector_rows(full, 3 * own)

    hat, norm_scale = moments(padded_rows(img_ref[...]))
    gain = vec[0:1]
    normed_t = (hat * gain + vec[1:2]).astype(BF16).T
    back = None
    for c in range(3):
        part = gtrip[:, c * width : (c + 1) * width]
        accw[c] += dot(normed_t, part)
        accv[2 + c : 3 + c] += jnp.sum(part.astype(F32), 0, keepdims=True)
        before = dot_nt(part, block_rows(full, c * own, own))
        back = before if back is None else back + before
    accv[0:1] += jnp.sum(back * hat, 0, keepdims=True)
    accv[1:2] += jnp.sum(back, 0, keepdims=True)
    grad_in = gres_ref[...].reshape(rows, width) + norm_backward(back, hat, norm_scale, gain)
    gin_ref[...] = unpadded(grad_in, group).astype(BF16)

    if last:

        @pl.when(step == pl.num_programs(0) - 1)
        def _():
            query = lax.broadcasted_iota(jnp.int32, (PAIR, PAIR), 0)
            other = lax.broadcasted_iota(jnp.int32, (PAIR, PAIR), 1)
            turn = jnp.where(query + other == PAIR - 1, 1.0, 0.0).astype(BF16)
            sums = []
            for h in range(heads):
                tile = accb[h // per, h % per * PAIR : (h % per + 1) * PAIR]
                high = tile.astype(BF16)
                low = (tile - high.astype(F32)).astype(BF16)
                back_to_front = dot(turn, jnp.concatenate([high, low], 1))
                back_to_front = back_to_front[:, :KEYS] + back_to_front[:, KEYS:]
                wide = jnp.concatenate([back_to_front, jnp.zeros_like(back_to_front)], 1)
                skewed = pltpu.roll(wide, 0, 1, stride=1, stride_axis=0)
                sums.append(jnp.sum(skewed, 0, keepdims=True))
            sums = pltpu.roll(jnp.concatenate(sums, 0), 2 * KEYS - PAIR + 1, 1)
            high = sums.astype(BF16)
            low = (sums - high.astype(F32)).astype(BF16)
            table = dot(high, choice_ref[...]) + dot(low, choice_ref[...])
            pieces = width // LANES
            vectors = jnp.concatenate(
                [
                    accv[v : v + 1, i * LANES : (i + 1) * LANES]
                    for v in (0, 1, 2, 4)
                    for i in range(pieces)
                ],
                0,
            )
            rest = width - table.shape[1] - LANES
            tile = jnp.concatenate([table, vectors, jnp.zeros((VEC_ROWS, rest), F32)], 1).astype(BF16)
            half = full.shape[0] // 2
            for number, ref in enumerate((keep_ref, send_ref)):

                def place(j, carry, ref=ref, number=number):
                    owner = ids_ref[number * half + j]
                    mine = pl.ds(pl.multiple_of(owner * own, own), own)
                    for c in range(3):
                        ref[j, c * own : (c + 1) * own] = accw[c, mine].astype(BF16)
                    ref[j, 3 * own : 3 * own + VEC_ROWS] = tile
                    return carry

                lax.fori_loop(0, half, place, 0)


def bias_kernel(table_ref, seen_ref, bias_ref):
    heads = table_ref.shape[0]
    per = bias_ref.shape[1] // PAIR
    for h in range(heads):
        row = jnp.broadcast_to(table_ref[h : h + 1], (PAIR, table_ref.shape[1]))
        skewed = pltpu.roll(row, 0, 1, stride=1, stride_axis=0)
        at = h % per * PAIR
        bias_ref[h // per, at : at + PAIR] = jnp.where(seen_ref[...] > 0, skewed[:, :KEYS], NEG)


def whole(shape):
    return pl.BlockSpec(shape, lambda *_: (0,) * len(shape))


def params(mib):
    return pltpu.CompilerParams(
        dimension_semantics=("arbitrary",), vmem_limit_bytes=mib * MIB
    )


def image_group(slots):
    return 2 if slots % 2 == 0 else 1


def split_steps(steps, shares):
    if steps < 2 * len(shares):
        return [steps]
    sizes = [max(1, int(steps * share + 0.5)) for share in shares[:-1]]
    return sizes + [steps - sum(sizes)]


ANY = pl.BlockSpec(memory_space=pl.ANY)
SMEM = pl.BlockSpec(memory_space=pltpu.SMEM)


def weight_scratch(pieces):
    owners = 2 * pieces[0].shape[0]
    shape = (owners,) + pieces[0].shape[1:]
    return [
        pltpu.VMEM(shape, BF16),
        pltpu.VMEM((VEC_ROWS, shape[-1]), F32),
    ], pltpu.SemaphoreType.DMA((owners,))


def attention_forward(ids, images, pieces, bias, heads, first, steps, group, carried):
    slots, width = images.shape[0], images.shape[-1]
    tokens = SIDE * COLS
    groups, stack = bias.shape[:2]
    block = lambda i: (first + i, 0, 0)
    block4 = lambda i: (first + i, 0, 0, 0)
    full, sems = weight_scratch(pieces)
    return pl.pallas_call(
        partial(forward_kernel, heads, len(carried)),
        grid=(steps,),
        in_specs=[
            SMEM,
            pl.BlockSpec((group, SIDE, SIDE, width), block4),
            ANY,
            ANY,
            whole(bias.shape),
        ]
        + [ANY] * len(carried),
        out_specs=[
            pl.BlockSpec((group, tokens, 3 * width), block),
            pl.BlockSpec((2 * group, groups, stack, KEYS), block4),
            pl.BlockSpec((2 * group, PAIR, width), block),
            pl.BlockSpec((2 * group, PAIR, width), block),
        ],
        out_shape=[
            jax.ShapeDtypeStruct((slots, tokens, 3 * width), BF16),
            jax.ShapeDtypeStruct((2 * slots, groups, stack, KEYS), BF16),
            jax.ShapeDtypeStruct((2 * slots, PAIR, width), BF16),
            jax.ShapeDtypeStruct((2 * slots, PAIR, width), F32),
        ],
        scratch_shapes=[pltpu.VMEM((group * tokens + COLS, 3 * width), BF16), *full, sems],
        input_output_aliases={5 + i: i for i in range(len(carried))},
        compiler_params=params(56),
        cost_estimate=pl.CostEstimate(
            flops=steps * group * tokens * width * width * 40,
            bytes_accessed=steps * group * 2 * MIB,
            transcendentals=0,
        ),
        name="attention_forward",
    )(ids, images, *pieces, bias, *carried)


def feed_forward(ids, counts, images, cotangent, mixed, inverse, pieces, chunks):
    slots, width = images.shape[0], images.shape[-1]
    group = next(g for g in (4, 2, 1) if slots % g == 0)
    tokens = SIDE * COLS
    image_spec = pl.BlockSpec((group, SIDE, SIDE, width), lambda i: (i, 0, 0, 0))
    row_spec = pl.BlockSpec((group, tokens, width), lambda i: (i, 0, 0))
    half = pieces[0].shape
    outs = [
        (images.shape, BF16, image_spec),
        ((slots, tokens, width), BF16, row_spec),
        ((slots, tokens, width), BF16, row_spec),
        (half, BF16, whole(half)),
        (half, BF16, whole(half)),
    ]
    full, sems = weight_scratch(pieces)
    return pl.pallas_call(
        mlp_kernel,
        grid=(slots // group,),
        in_specs=[SMEM, SMEM, image_spec, image_spec, row_spec, row_spec, ANY, ANY],
        out_specs=[o[2] for o in outs],
        out_shape=[jax.ShapeDtypeStruct(o[0], o[1]) for o in outs],
        scratch_shapes=[
            *full,
            pltpu.VMEM((chunks, width, width), F32),
            pltpu.VMEM((chunks, width, width), F32),
            pltpu.VMEM((width, width), F32),
            pltpu.VMEM((8, width), F32),
            pltpu.VMEM((8, width), F32),
            pltpu.VMEM((chunks * width, width), BF16),
            sems,
        ],
        compiler_params=params(62),
        cost_estimate=pl.CostEstimate(
            flops=slots * tokens * width * width * (3 + chunks * 6) * 4,
            bytes_accessed=32 * MIB,
            transcendentals=0,
        ),
        name="feed_forward",
    )(ids, counts, images, cotangent, mixed, inverse, *pieces)


def attention_backward(
    ids, images, gres, gmix, mixed, triple, probs, pieces, choice, heads, first, steps, group,
    carried, last,
):
    slots, width = images.shape[0], images.shape[-1]
    tokens = SIDE * COLS
    groups, stack = probs.shape[1:3]
    block = lambda i: (first + i, 0, 0)
    block4 = lambda i: (first + i, 0, 0, 0)
    image_spec = pl.BlockSpec((group, SIDE, SIDE, width), block4)
    sums = [(3, width, width), (8, width), (groups, stack, KEYS)]
    half = pieces[0].shape
    outs = [(s, F32) for s in sums] if not last else [(half, BF16), (half, BF16)]
    full, sems = weight_scratch(pieces)
    return pl.pallas_call(
        partial(backward_kernel, heads, not carried, last),
        grid=(steps,),
        in_specs=[
            SMEM,
            image_spec,
            pl.BlockSpec((group, tokens, width), block),
            pl.BlockSpec((2 * group, PAIR, width), block),
            pl.BlockSpec((2 * group, PAIR, width), block),
            pl.BlockSpec((group, tokens, 3 * width), block),
            pl.BlockSpec((2 * group, groups, stack, KEYS), block4),
            ANY,
            ANY,
            whole(choice.shape),
        ]
        + ([ANY] + [whole(s) for s in sums] if carried else []),
        out_specs=[image_spec] + [whole(s) for s, _ in outs],
        out_shape=[jax.ShapeDtypeStruct(images.shape, BF16)]
        + [jax.ShapeDtypeStruct(s, k) for s, k in outs],
        scratch_shapes=([pltpu.VMEM(s, F32) for s in sums] if last else [])
        + [
            pltpu.VMEM((group * tokens + COLS, 3 * width), BF16),
            pltpu.VMEM((group * tokens, 3 * width), BF16),
            *full,
            sems,
        ],
        input_output_aliases={10: 0} if carried else {},
        compiler_params=params(62),
        cost_estimate=pl.CostEstimate(
            flops=steps * group * tokens * width * width * 90,
            bytes_accessed=steps * group * 4 * MIB,
            transcendentals=0,
        ),
        name="attention_backward",
    )(ids, images, gres, gmix, mixed, triple, probs, *pieces, choice, *carried)


def expand_bias(table, seen, heads, per):
    return pl.pallas_call(
        bias_kernel,
        out_shape=jax.ShapeDtypeStruct((heads // per, per * PAIR, KEYS), F32),
        name="expand_bias",
    )(table, seen)


def flip(values, bits, devices):
    return lax.ppermute(values, "dev", [(i, i ^ bits) for i in range(devices)])


def exchange_groups(devices):
    bits = [1 << i for i in range(devices.bit_length() - 1)]
    return [bits[:1]] + [bits[i : i + 2] for i in range(1, len(bits), 2)]


def mixes(group):
    found = [0]
    for bit in group:
        found = found + [f ^ bit for f in found]
    return found


def block_order(devices):
    order = [0]
    for group in exchange_groups(devices)[:0:-1]:
        order = [m ^ o for m in mixes(group) for o in order]
    return order + [exchange_groups(devices)[0][0] ^ o for o in order]


def gather_parts(held, group, devices):
    return [held] + [flip(held, m, devices) for m in mixes(group)[1:]]


def gather_group(held, group, devices):
    return jnp.concatenate(gather_parts(held, group, devices))


def share_parts(held, group, devices):
    parts = jnp.split(held, 2 ** len(group))
    return parts[:1] + [flip(part, m, devices) for part, m in zip(parts[1:], mixes(group)[1:])]


def add_parts(parts):
    sums = [part.astype(F32) for part in parts]
    while len(sums) > 1:
        sums = [a + b for a, b in zip(sums[::2], sums[1::2])]
    return sums[0]


def tie(first, second):
    return lax.optimization_barrier((first, second))


def offsets():
    picks = np.full((2 * KEYS,), -1, np.int64)
    area = WINDOW * WINDOW
    for i in range(area):
        for j in range(area):
            place = (j // WINDOW - i // WINDOW) * COLS + j % WINDOW - i % WINDOW
            picks[place % (2 * KEYS)] = i * area + j
    return picks


def seen_keys():
    place = np.arange(KEYS)
    row, col = place // COLS, place % COLS
    side = np.where(col < SIDE, col // WINDOW, 2)
    ok = (row < WINDOW) & (side < 2)
    seen = (side[:PAIR, None] == side[None]) & ok[:PAIR, None] & ok[None]
    return seen.astype(np.float32)


def owner_lanes(vectors, me, devices):
    share = vectors.shape[-1]
    lane = lax.broadcasted_iota(jnp.int32, (1, share * devices), 1)
    return jnp.where(lane // share == me, jnp.tile(vectors, (1, devices)), 0)


def regroup(pieces, order, fields, me, devices, owners):
    by_number = np.argsort(np.array(order))
    blocks = jnp.concatenate(pieces)
    blocks = jnp.take(blocks, jnp.asarray(by_number)[jnp.arange(devices) ^ me], axis=0)
    out, at = [], 0
    for rows in fields:
        out.append(blocks[:, at : at + rows].reshape(owners, -1, blocks.shape[-1]))
        at += rows
    vectors = blocks[:, at:].reshape(owners, devices // owners, VEC_ROWS, -1)
    out.append(jnp.sum(vectors.astype(F32), 1).astype(BF16))
    return jnp.split(jnp.concatenate(out, 1), 2)


def ungroup(pieces, order, fields, me, devices, owners):
    blocks = jnp.concatenate(pieces)
    many = devices // owners
    out, at = [], 0
    for rows in fields:
        rows = rows * many
        out.append(blocks[:, at : at + rows].reshape(devices, rows // many, -1))
        at += rows
    out.append(jnp.repeat(blocks[:, at:], many, axis=0))
    blocks = jnp.take(jnp.concatenate(out, 1), jnp.asarray(np.array(order)) ^ me, axis=0)
    return jnp.split(blocks, 2)


def shards(
    devices,
    images,
    cotangent,
    image_counts,
    rel_index,
    ln1_gain,
    ln1_shift,
    w_qkv,
    q_bias,
    v_bias,
    w_proj,
    b_proj,
    ln2_gain,
    ln2_shift,
    w_fc1,
    b_fc1,
    w_fc2,
    b_fc2,
    bias_table,
):
    me = lax.axis_index("dev")
    slots, width = images.shape[0], images.shape[3]
    table_rows, heads = bias_table.shape
    own = ln1_gain.shape[0]
    span = b_fc1.shape[0]
    chunks = span // own
    per = LANES // (width // heads)
    groups = exchange_groups(devices)
    order = block_order(devices)
    aligned = own % COLS == 0
    owners = devices if aligned else width // COLS
    attn_fields = [own] * 3
    mlp_fields = [span] + [own] * (chunks + 1)
    if aligned:
        ids = jnp.asarray(np.array(order, np.int32)) ^ me
    else:
        ids = jnp.arange(owners, dtype=jnp.int32)

    attn_vec = owner_lanes(jnp.stack([ln1_gain, ln1_shift, q_bias, v_bias]), me, devices)
    attn_block = jnp.concatenate(
        [w_qkv[:, c * width : (c + 1) * width] for c in range(3)]
        + [attn_vec, jnp.zeros((VEC_ROWS - 4, width), BF16)]
    )
    mlp_vec = owner_lanes(jnp.stack([b_proj, ln2_gain, ln2_shift, b_fc2]), me, devices)
    hidden_vec = owner_lanes(b_fc1[None], me, devices).reshape(chunks, width)
    mlp_block = jnp.concatenate(
        [w_fc2]
        + [w_fc1[:, c * width : (c + 1) * width] for c in range(chunks)]
        + [w_proj, mlp_vec, hidden_vec, jnp.zeros((VEC_ROWS - 4 - chunks, width), BF16)]
    )
    far = groups[:0:-1]

    picks = offsets()
    rows_of = rel_index.reshape(-1)[np.maximum(picks, 0)]
    rows_of = jnp.where(jnp.asarray(picks) >= 0, rows_of, -1)
    choice = (rows_of[:, None] == jnp.arange(2 * KEYS, dtype=jnp.int32)).astype(BF16)
    table = jnp.pad(bias_table, ((0, 2 * KEYS - table_rows), (0, 0))).T
    high = table.astype(BF16)
    mid = (table - high.astype(F32)).astype(BF16)
    low = (table - high.astype(F32) - mid.astype(F32)).astype(BF16)
    by_offset = dot_nt(jnp.concatenate([high, mid, low]), choice)
    by_offset = by_offset[:heads] + by_offset[heads : 2 * heads] + by_offset[2 * heads :]
    bias = expand_bias(by_offset, jnp.asarray(seen_keys()), heads, per)

    attn_held, mlp_held = attn_block[None], mlp_block[None]
    for bits in far[:-1]:
        attn_held = gather_group(attn_held, bits, devices)
        attn_held, mlp_held = tie(attn_held, mlp_held)
        mlp_held = gather_group(mlp_held, bits, devices)
    attn_held = gather_group(attn_held, far[-1], devices)
    attn_held, mlp_held = tie(attn_held, mlp_held)
    bias, attn_held = tie(bias, attn_held)
    attn_pieces = (attn_held, flip(attn_held, groups[0][0], devices))
    if not aligned:
        attn_pieces = regroup(attn_pieces, order, attn_fields, me, devices, owners)

    group = image_group(slots)
    sizes = split_steps(slots // group, (2 / 3, 1 / 3))
    mlp_parts = gather_parts(mlp_held, far[-1], devices)
    carried, first = (), 0
    for steps in sizes:
        if carried:
            carried, mlp_parts = tie(carried, mlp_parts)
        carried = attention_forward(
            ids, images, attn_pieces, bias, heads, first, steps, group, carried
        )
        first += steps
    mlp_held = jnp.concatenate(mlp_parts)
    triple, raised, mixed, inverse = carried
    mlp_pieces = (mlp_held, flip(mlp_held, groups[0][0], devices))
    if not aligned:
        mlp_pieces = regroup(mlp_pieces, order, mlp_fields, me, devices, owners)
    output, gres, gmix, *mlp_sums = feed_forward(
        ids,
        image_counts,
        images,
        cotangent,
        mixed.reshape(slots, SIDE * COLS, width),
        inverse.reshape(slots, SIDE * COLS, width),
        mlp_pieces,
        chunks,
    )

    if not aligned:
        mlp_sums = ungroup(mlp_sums, order, mlp_fields, me, devices, owners)
    gmix = gmix.reshape(2 * slots, PAIR, width)
    sizes = split_steps(slots // group, (1 / 6, 1 / 2, 1 / 3))
    left = groups[1:]
    parts = [mlp_sums[0], flip(mlp_sums[1], groups[0][0], devices)]
    carried, first = (), 0
    for call, steps in enumerate(sizes):
        if carried:
            carried, parts = tie(carried, parts)
            if left:
                parts = share_parts(add_parts(parts).astype(BF16), left[0], devices)
                left = left[1:]
        carried = attention_backward(
            ids, images, gres, gmix, mixed, triple, raised, attn_pieces, choice, heads, first,
            steps, group, tuple(carried), call == len(sizes) - 1,
        )
        first += steps
    for bits in left:
        parts = share_parts(add_parts(parts).astype(BF16), bits, devices)
    if len(sizes) > 1:
        carried, parts = tie(carried, parts)
    mlp_mine = add_parts(parts).reshape(-1, width)

    grad_input, *attn_sums = carried
    if not aligned:
        attn_sums = ungroup(attn_sums, order, attn_fields, me, devices, owners)
    mine = add_parts([attn_sums[0], flip(attn_sums[1], groups[0][0], devices)])
    for bits in groups[1:]:
        mine = add_parts(share_parts(mine.astype(BF16), bits, devices))
    mine = mine.reshape(-1, width)

    grad_fc2 = mlp_mine[:span]
    at = span
    grad_fc1 = jnp.concatenate(
        [mlp_mine[at + c * own : at + (c + 1) * own] for c in range(chunks)], 1
    )
    at += chunks * own
    grad_proj = mlp_mine[at : at + own]
    at += own
    vectors = lax.dynamic_slice_in_dim(mlp_mine[at : at + 4], me * own, own, 1)
    grad_proj_bias, grad_gain_two, grad_shift_two, grad_fc2_bias = vectors
    grad_fc1_bias = lax.dynamic_slice_in_dim(
        mlp_mine[at + 4 : at + 4 + chunks].reshape(-1), me * span, span, 0
    )

    grad_qkv = jnp.concatenate([mine[c * own : (c + 1) * own] for c in range(3)], 1)
    tile = mine[3 * own :]
    table_total = tile[:heads, :table_rows].T
    vectors = tile[:, 2 * KEYS : 2 * KEYS + LANES].reshape(4, width)
    vectors = lax.dynamic_slice_in_dim(vectors, me * own, own, 1)
    grad_gain_one, grad_shift_one, grad_query_bias, grad_value_bias = vectors
    return (
        output,
        grad_input,
        grad_gain_one,
        grad_shift_one,
        grad_qkv,
        grad_query_bias,
        grad_value_bias,
        grad_proj,
        grad_proj_bias,
        grad_gain_two,
        grad_shift_two,
        grad_fc1,
        grad_fc1_bias,
        grad_fc2,
        grad_fc2_bias,
        table_total,
    )


def solution(mesh):
    rows = P("dev", None)
    image = P("dev", None, None, None)
    flat = P("dev")
    in_specs = (
        image, image, flat, P(), flat, flat, rows, flat, flat, rows, flat,
        flat, flat, rows, flat, rows, flat, P(),
    )
    out_specs = (
        image, image, flat, flat, rows, flat, flat, rows, flat,
        flat, flat, rows, flat, rows, flat, P(),
    )
    body = partial(shards, mesh.shape["dev"])
    return jax.shard_map(body, mesh=mesh, in_specs=in_specs, out_specs=out_specs, check_vma=False)
```

```python
from functools import partial

import jax
import jax.numpy as jnp
import numpy as np
from jax import lax
from jax.experimental import pallas as pl
from jax.experimental.pallas import tpu as pltpu
from jax.sharding import PartitionSpec as P

WINDOW = 7
SIDE = 14
COLS = 16
PAIR = WINDOW * COLS
KEYS = 128
LANES = 128
EPSILON = 1e-05
HIGHEST = lax.Precision.HIGHEST
MIB = 2**20
NEG = -1e30
VEC_ROWS = 16
UNROLL = 4
F32 = jnp.float32
BF16 = jnp.bfloat16


def dot(left, right):
    return lax.dot_general(left, right, (((1,), (0,)), ((), ())), preferred_element_type=F32)


def dot_nt(left, right):
    return lax.dot_general(left, right, (((1,), (1,)), ((), ())), preferred_element_type=F32)


def dot_tn(left, right):
    return lax.dot_general(left, right, (((0,), (0,)), ((), ())), preferred_element_type=F32)


def padded_rows(block):
    wide = block.astype(F32)
    wide = jnp.pad(wide, ((0, 0), (0, 0), (0, COLS - SIDE), (0, 0)))
    return wide.reshape(-1, block.shape[-1])


def unpadded(rows, images):
    return rows.reshape(images, SIDE, COLS, rows.shape[-1])[:, :, :SIDE, :]


def moments(values):
    center = values - jnp.mean(values, -1, keepdims=True)
    spread = jnp.mean(center * center, -1, keepdims=True)
    scale = lax.rsqrt(spread + EPSILON)
    return center * scale, scale


def norm_backward(grad, hat, scale, gain):
    inner = grad * gain
    mean_one = jnp.mean(inner, -1, keepdims=True)
    mean_two = jnp.mean(inner * hat, -1, keepdims=True)
    return scale * (inner - mean_one - hat * mean_two)


def head_masks(head_dim):
    lane = lax.broadcasted_iota(jnp.int32, (1, LANES), 1) // head_dim
    return [lane == h for h in range(LANES // head_dim)]


def stacked(block, masks):
    zero = jnp.zeros_like(block)
    return jnp.concatenate([jnp.where(m, block, zero) for m in masks], 0)


def side_by_side(tall, parts):
    rows = tall.shape[0] // parts
    return jnp.concatenate([tall[i * rows : (i + 1) * rows] for i in range(parts)], 1)


def fetch(ids_ref, pieces, full, sems):
    copies = []
    for number, piece in enumerate(pieces):
        count = piece.shape[0]
        for j in range(count):
            at = number * count + j
            copies.append(
                pltpu.make_async_copy(piece.at[j], full.at[ids_ref[at]], sems.at[at])
            )
    return copies


def block_rows(full, start, rows):
    part = full[:, start : start + rows, :]
    return part.reshape(-1, part.shape[-1])


def vector_rows(full, start):
    return jnp.sum(full[:, start : start + VEC_ROWS, :].astype(F32), 0)


def head_pairs(heads):
    return [slice(h, min(h + 2, heads)) for h in range(0, heads, 2)]


def own_blocks(products, parts):
    rows, lanes = products.shape[0] // parts, products.shape[1] // parts
    return jnp.concatenate(
        [products[i * rows : (i + 1) * rows, i * lanes : (i + 1) * lanes] for i in range(parts)], 0
    )


def forward_kernel(heads, carried, ids_ref, img_ref, one_ref, two_ref, bias_ref, *refs):
    triple_ref, raised_ref, mixed_ref, inverse_ref, trip, full, vec, sems = refs[carried:]
    group = img_ref.shape[0]
    width = img_ref.shape[-1]
    head_dim = width // heads
    scale = head_dim ** (-0.5)
    per = LANES // head_dim
    rows = group * SIDE * COLS
    own = width // full.shape[0]

    @pl.when(pl.program_id(0) == 0)
    def _():
        copies = fetch(ids_ref, (one_ref, two_ref), full, sems)
        for copy in copies:
            copy.start()
        for copy in copies:
            copy.wait()
        vec[...] = vector_rows(full, 3 * own)

    ones = stacked(jnp.ones((KEYS, LANES), BF16), head_masks(head_dim))
    inputs = padded_rows(img_ref[...])
    hat, _ = moments(inputs)
    normed = (hat * vec[0:1] + vec[1:2]).astype(BF16)
    trip[rows:, :] = jnp.zeros((COLS, 3 * width), BF16)
    for c, extra in enumerate((vec[2:3], None, vec[3:4])):
        part = dot(normed, block_rows(full, c * own, own))
        if extra is not None:
            part = part + extra
        part = part.astype(BF16)
        trip[0:rows, c * width : (c + 1) * width] = part
        triple_ref[:, :, c * width : (c + 1) * width] = part.reshape(group, SIDE * COLS, width)
    masks = head_masks(head_dim)

    def pair(p, carry):
        start = pl.multiple_of(p * PAIR, COLS)
        for g in range(width // LANES):
            q = trip[pl.ds(start, PAIR), g * LANES : (g + 1) * LANES]
            k = trip[pl.ds(start, KEYS), width + g * LANES : width + (g + 1) * LANES]
            v = trip[pl.ds(start, KEYS), 2 * width + g * LANES : 2 * width + (g + 1) * LANES]
            tiles = []
            for some in head_pairs(per):
                part = slice(some.start * PAIR, some.stop * PAIR)
                scores = dot_nt(stacked(q, masks[some]), k) * scale + bias_ref[g, part]
                top = jnp.max(scores, -1, keepdims=True)
                tiles.append(jnp.exp(scores - top).astype(BF16))
                raised_ref[p, g, part] = tiles[-1]
            raised = jnp.concatenate(tiles, 0)
            both = dot(side_by_side(raised, per), jnp.concatenate([stacked(v, masks), ones], 1))
            inverse = 1.0 / both[:, LANES:]
            inverse_ref[p, :, g * LANES : (g + 1) * LANES] = inverse
            mixed = (both[:, :LANES] * inverse).astype(BF16)
            mixed_ref[p, :, g * LANES : (g + 1) * LANES] = mixed
        return carry

    lax.fori_loop(0, 2 * group, pair, 0, unroll=UNROLL)


def mlp_kernel(
    ids_ref, counts_ref, img_ref, cot_ref, mixed_ref, inverse_ref, one_ref, two_ref,
    out_ref, gres_ref, gmix_ref, keep_ref, send_ref,
    full, vec, acc1, acc2, accp, accv, accb, turned, sems,
):
    step = pl.program_id(0)
    group = img_ref.shape[0]
    width = img_ref.shape[-1]
    rows = group * SIDE * COLS
    chunks = acc1.shape[0]
    owners = full.shape[0]
    own = width // owners
    span = chunks * own
    at_one, at_proj, at_vec = span, 2 * span, 2 * span + own

    @pl.when(step == 0)
    def _():
        copies = fetch(ids_ref, (one_ref, two_ref), full, sems)
        for copy in copies:
            copy.start()
        for ref in (acc1, acc2, accp, accv, accb):
            ref[...] = jnp.zeros_like(ref)
        for copy in copies:
            copy.wait()
        vec[...] = vector_rows(full, at_vec)

    row = lax.broadcasted_iota(jnp.int32, (rows, 1), 0)
    image = row // (SIDE * COLS)
    live = ((step * group + image) < counts_ref[0]) & (row % COLS < SIDE)
    mixed = mixed_ref[...].reshape(rows, width)
    w_proj = block_rows(full, at_proj, own)
    residual = padded_rows(img_ref[...]) + dot(mixed, w_proj) + vec[0:1]
    hat, scale = moments(residual)
    gain = vec[1:2]
    normed = (hat * gain + vec[2:3]).astype(BF16)
    normed_t = normed.T
    grad_out = jnp.where(live, padded_rows(cot_ref[...]), 0.0)
    grad_low = grad_out.astype(BF16)
    grad_low_t = grad_low.T
    total, back = None, None
    for c in range(chunks):
        w1 = block_rows(full, at_one + c * own, own)
        half = owners // chunks
        w2 = full[c * half : (c + 1) * half, :span, :].reshape(width, width)
        hidden = dot(normed, w1) + vec[4 + c : 5 + c]
        below = 0.5 + 0.5 * lax.erf(hidden * (0.5**0.5))
        act = (hidden * below).astype(BF16)
        slope = below + hidden * (0.3989422804014327 * jnp.exp(-0.5 * hidden * hidden))
        after = dot(act, w2)
        total = after if total is None else total + after
        grad_hidden = (slope * dot_nt(grad_low, w2)).astype(BF16)
        before = dot_nt(grad_hidden, w1)
        back = before if back is None else back + before
        acc1[c] += dot(normed_t, grad_hidden)
        acc2[c] += dot(grad_low_t, act)
        accb[c : c + 1] += jnp.sum(grad_hidden.astype(F32), 0, keepdims=True)
    result = jnp.where(live, residual + total + vec[3:4], 0.0)
    out_ref[...] = unpadded(result, group).astype(BF16)
    grad_res = grad_out + norm_backward(back, hat, scale, gain)
    grad_res_low = grad_res.astype(BF16)
    gres_ref[...] = grad_res_low.reshape(group, SIDE * COLS, width)
    grad_mixed = dot_nt(grad_res_low, w_proj) * inverse_ref[...].reshape(rows, width)
    gmix_ref[...] = grad_mixed.astype(BF16).reshape(group, SIDE * COLS, width)
    accp[...] += dot(mixed.T, grad_res_low)
    accv[0:1] += jnp.sum(grad_res_low.astype(F32), 0, keepdims=True)
    accv[1:2] += jnp.sum(back * hat, 0, keepdims=True)
    accv[2:3] += jnp.sum(back, 0, keepdims=True)
    accv[3:4] += jnp.sum(grad_low.astype(F32), 0, keepdims=True)

    @pl.when(step == pl.num_programs(0) - 1)
    def _():
        for c in range(chunks):
            turned[c * width : (c + 1) * width] = acc2[c].astype(BF16).T
        sums = jnp.concatenate([accv[0:4], accb[0:4], jnp.zeros((8, width), F32)], 0).astype(BF16)
        half = owners // 2
        for number, ref in enumerate((keep_ref, send_ref)):

            def place(j, carry, ref=ref, number=number):
                owner = ids_ref[number * half + j]
                ref[j, 0:span] = turned[pl.ds(pl.multiple_of(owner * span, span), span)]
                mine = pl.ds(pl.multiple_of(owner * own, own), own)
                for c in range(chunks):
                    ref[j, at_one + c * own : at_one + (c + 1) * own] = acc1[c, mine].astype(BF16)
                ref[j, at_proj : at_proj + own] = accp[mine].astype(BF16)
                ref[j, at_vec : at_vec + VEC_ROWS] = sums
                return carry

            lax.fori_loop(0, half, place, 0)


def backward_kernel(
    heads, first, last, ids_ref, img_ref, gres_ref, gmix_ref, mixed_ref, triple_ref, raised_ref,
    one_ref, two_ref, choice_ref, *refs
):
    trip, gtrip, full, vec, sems = refs[-5:]
    step = pl.program_id(0)
    group = img_ref.shape[0]
    width = img_ref.shape[-1]
    head_dim = width // heads
    scale = head_dim ** (-0.5)
    per = LANES // head_dim
    rows = group * SIDE * COLS
    own = width // full.shape[0]
    carried = () if first else refs[1:4]
    outs = refs[0 if first else 4 : -5]
    gin_ref = outs[0]
    if last:
        keep_ref, send_ref, accw, accv, accb = outs[1:]
    else:
        accw, accv, accb = outs[1:]
    copies = fetch(ids_ref, (one_ref, two_ref), full, sems)

    @pl.when(step == 0)
    def _():
        for copy in copies:
            copy.start()
        if carried:
            accw[...] = carried[0][...]
            accv[...] = carried[1][...]
            accb[...] = carried[2][...]
        else:
            accw[...] = jnp.zeros_like(accw)
            accv[...] = jnp.zeros_like(accv)
            accb[...] = jnp.zeros_like(accb)

    trip[0:rows, :] = triple_ref[...].reshape(rows, 3 * width)
    trip[rows:, :] = jnp.zeros((COLS, 3 * width), BF16)
    masks = head_masks(head_dim)
    ones = jnp.ones((KEYS, LANES), BF16)

    def pair(p, carry):
        start = pl.multiple_of(p * PAIR, COLS)
        for g in range(width // LANES):
            lo, hi = g * LANES, (g + 1) * LANES
            q = trip[pl.ds(start, PAIR), lo:hi]
            k = trip[pl.ds(start, KEYS), width + lo : width + hi]
            v = trip[pl.ds(start, KEYS), 2 * width + lo : 2 * width + hi]
            raised = raised_ref[p, g]
            grad_mixed = gmix_ref[p, :, lo:hi]
            inner = -(grad_mixed.astype(F32) * mixed_ref[p, :, lo:hi].astype(F32))
            inner = inner.astype(BF16)
            right = jnp.concatenate([v, ones], 1)
            tiles = []
            for some in head_pairs(per):
                part = slice(some.start * PAIR, some.stop * PAIR)
                left = [stacked(grad_mixed, masks[some]), stacked(inner, masks[some])]
                grad_probs = dot_nt(jnp.concatenate(left, 1), right)
                tiles.append((raised_ref[p, g, part].astype(F32) * grad_probs).astype(BF16))
                accb[g, part] += tiles[-1].astype(F32)
            grad_scores = jnp.concatenate(tiles, 0)
            wide = side_by_side(grad_scores, per)
            grad_q = dot(wide, stacked(k, masks)) * scale
            grad_k = own_blocks(dot(q.T, wide), per) * scale
            grad_v = own_blocks(dot(grad_mixed.T, side_by_side(raised, per)), per)
            gtrip[pl.ds(start, PAIR), lo:hi] = grad_q.astype(BF16)
            gtrip[pl.ds(start, PAIR), width + lo : width + hi] = grad_k.astype(BF16).T[:PAIR]
            gtrip[pl.ds(start, PAIR), 2 * width + lo : 2 * width + hi] = grad_v.astype(BF16).T[:PAIR]
        return carry

    lax.fori_loop(0, 2 * group, pair, 0, unroll=UNROLL)

    @pl.when(step == 0)
    def _():
        for copy in copies:
            copy.wait()
        vec[...] = vector_rows(full, 3 * own)

    hat, norm_scale = moments(padded_rows(img_ref[...]))
    gain = vec[0:1]
    normed_t = (hat * gain + vec[1:2]).astype(BF16).T
    back = None
    for c in range(3):
        part = gtrip[:, c * width : (c + 1) * width]
        accw[c] += dot(normed_t, part)
        accv[2 + c : 3 + c] += jnp.sum(part.astype(F32), 0, keepdims=True)
        before = dot_nt(part, block_rows(full, c * own, own))
        back = before if back is None else back + before
    accv[0:1] += jnp.sum(back * hat, 0, keepdims=True)
    accv[1:2] += jnp.sum(back, 0, keepdims=True)
    grad_in = gres_ref[...].reshape(rows, width) + norm_backward(back, hat, norm_scale, gain)
    gin_ref[...] = unpadded(grad_in, group).astype(BF16)

    if last:

        @pl.when(step == pl.num_programs(0) - 1)
        def _():
            query = lax.broadcasted_iota(jnp.int32, (PAIR, PAIR), 0)
            other = lax.broadcasted_iota(jnp.int32, (PAIR, PAIR), 1)
            turn = jnp.where(query + other == PAIR - 1, 1.0, 0.0).astype(BF16)
            sums = []
            for h in range(heads):
                tile = accb[h // per, h % per * PAIR : (h % per + 1) * PAIR]
                high = tile.astype(BF16)
                low = (tile - high.astype(F32)).astype(BF16)
                back_to_front = dot(turn, jnp.concatenate([high, low], 1))
                back_to_front = back_to_front[:, :KEYS] + back_to_front[:, KEYS:]
                wide = jnp.concatenate([back_to_front, jnp.zeros_like(back_to_front)], 1)
                skewed = pltpu.roll(wide, 0, 1, stride=1, stride_axis=0)
                sums.append(jnp.sum(skewed, 0, keepdims=True))
            sums = pltpu.roll(jnp.concatenate(sums, 0), 2 * KEYS - PAIR + 1, 1)
            high = sums.astype(BF16)
            low = (sums - high.astype(F32)).astype(BF16)
            table = dot(high, choice_ref[...]) + dot(low, choice_ref[...])
            pieces = width // LANES
            vectors = jnp.concatenate(
                [
                    accv[v : v + 1, i * LANES : (i + 1) * LANES]
                    for v in (0, 1, 2, 4)
                    for i in range(pieces)
                ],
                0,
            )
            rest = width - table.shape[1] - LANES
            tile = jnp.concatenate([table, vectors, jnp.zeros((VEC_ROWS, rest), F32)], 1).astype(BF16)
            half = full.shape[0] // 2
            for number, ref in enumerate((keep_ref, send_ref)):

                def place(j, carry, ref=ref, number=number):
                    owner = ids_ref[number * half + j]
                    mine = pl.ds(pl.multiple_of(owner * own, own), own)
                    for c in range(3):
                        ref[j, c * own : (c + 1) * own] = accw[c, mine].astype(BF16)
                    ref[j, 3 * own : 3 * own + VEC_ROWS] = tile
                    return carry

                lax.fori_loop(0, half, place, 0)


def bias_kernel(table_ref, seen_ref, bias_ref):
    heads = table_ref.shape[0]
    per = bias_ref.shape[1] // PAIR
    for h in range(heads):
        row = jnp.broadcast_to(table_ref[h : h + 1], (PAIR, table_ref.shape[1]))
        skewed = pltpu.roll(row, 0, 1, stride=1, stride_axis=0)
        at = h % per * PAIR
        bias_ref[h // per, at : at + PAIR] = jnp.where(seen_ref[...] > 0, skewed[:, :KEYS], NEG)


def whole(shape):
    return pl.BlockSpec(shape, lambda *_: (0,) * len(shape))


def params(mib):
    return pltpu.CompilerParams(
        dimension_semantics=("arbitrary",), vmem_limit_bytes=mib * MIB
    )


def image_group(slots):
    return 2 if slots % 2 == 0 else 1


def split_steps(steps, shares):
    if steps < 2 * len(shares):
        return [steps]
    sizes = [max(1, int(steps * share + 0.5)) for share in shares[:-1]]
    return sizes + [steps - sum(sizes)]


ANY = pl.BlockSpec(memory_space=pl.ANY)
SMEM = pl.BlockSpec(memory_space=pltpu.SMEM)


def weight_scratch(pieces):
    owners = 2 * pieces[0].shape[0]
    shape = (owners,) + pieces[0].shape[1:]
    return [
        pltpu.VMEM(shape, BF16),
        pltpu.VMEM((VEC_ROWS, shape[-1]), F32),
    ], pltpu.SemaphoreType.DMA((owners,))


def attention_forward(ids, images, pieces, bias, heads, first, steps, group, carried):
    slots, width = images.shape[0], images.shape[-1]
    tokens = SIDE * COLS
    groups, stack = bias.shape[:2]
    block = lambda i: (first + i, 0, 0)
    block4 = lambda i: (first + i, 0, 0, 0)
    full, sems = weight_scratch(pieces)
    return pl.pallas_call(
        partial(forward_kernel, heads, len(carried)),
        grid=(steps,),
        in_specs=[
            SMEM,
            pl.BlockSpec((group, SIDE, SIDE, width), block4),
            ANY,
            ANY,
            whole(bias.shape),
        ]
        + [ANY] * len(carried),
        out_specs=[
            pl.BlockSpec((group, tokens, 3 * width), block),
            pl.BlockSpec((2 * group, groups, stack, KEYS), block4),
            pl.BlockSpec((2 * group, PAIR, width), block),
            pl.BlockSpec((2 * group, PAIR, width), block),
        ],
        out_shape=[
            jax.ShapeDtypeStruct((slots, tokens, 3 * width), BF16),
            jax.ShapeDtypeStruct((2 * slots, groups, stack, KEYS), BF16),
            jax.ShapeDtypeStruct((2 * slots, PAIR, width), BF16),
            jax.ShapeDtypeStruct((2 * slots, PAIR, width), F32),
        ],
        scratch_shapes=[pltpu.VMEM((group * tokens + COLS, 3 * width), BF16), *full, sems],
        input_output_aliases={5 + i: i for i in range(len(carried))},
        compiler_params=params(56),
        cost_estimate=pl.CostEstimate(
            flops=steps * group * tokens * width * width * 40,
            bytes_accessed=steps * group * 2 * MIB,
            transcendentals=0,
        ),
        name="attention_forward",
    )(ids, images, *pieces, bias, *carried)


def feed_forward(ids, counts, images, cotangent, mixed, inverse, pieces, chunks):
    slots, width = images.shape[0], images.shape[-1]
    group = next(g for g in (4, 2, 1) if slots % g == 0)
    tokens = SIDE * COLS
    image_spec = pl.BlockSpec((group, SIDE, SIDE, width), lambda i: (i, 0, 0, 0))
    row_spec = pl.BlockSpec((group, tokens, width), lambda i: (i, 0, 0))
    half = pieces[0].shape
    outs = [
        (images.shape, BF16, image_spec),
        ((slots, tokens, width), BF16, row_spec),
        ((slots, tokens, width), BF16, row_spec),
        (half, BF16, whole(half)),
        (half, BF16, whole(half)),
    ]
    full, sems = weight_scratch(pieces)
    return pl.pallas_call(
        mlp_kernel,
        grid=(slots // group,),
        in_specs=[SMEM, SMEM, image_spec, image_spec, row_spec, row_spec, ANY, ANY],
        out_specs=[o[2] for o in outs],
        out_shape=[jax.ShapeDtypeStruct(o[0], o[1]) for o in outs],
        scratch_shapes=[
            *full,
            pltpu.VMEM((chunks, width, width), F32),
            pltpu.VMEM((chunks, width, width), F32),
            pltpu.VMEM((width, width), F32),
            pltpu.VMEM((8, width), F32),
            pltpu.VMEM((8, width), F32),
            pltpu.VMEM((chunks * width, width), BF16),
            sems,
        ],
        compiler_params=params(62),
        cost_estimate=pl.CostEstimate(
            flops=slots * tokens * width * width * (3 + chunks * 6) * 4,
            bytes_accessed=32 * MIB,
            transcendentals=0,
        ),
        name="feed_forward",
    )(ids, counts, images, cotangent, mixed, inverse, *pieces)


def attention_backward(
    ids, images, gres, gmix, mixed, triple, probs, pieces, choice, heads, first, steps, group,
    carried, last,
):
    slots, width = images.shape[0], images.shape[-1]
    tokens = SIDE * COLS
    groups, stack = probs.shape[1:3]
    block = lambda i: (first + i, 0, 0)
    block4 = lambda i: (first + i, 0, 0, 0)
    image_spec = pl.BlockSpec((group, SIDE, SIDE, width), block4)
    sums = [(3, width, width), (8, width), (groups, stack, KEYS)]
    half = pieces[0].shape
    outs = [(s, F32) for s in sums] if not last else [(half, BF16), (half, BF16)]
    full, sems = weight_scratch(pieces)
    return pl.pallas_call(
        partial(backward_kernel, heads, not carried, last),
        grid=(steps,),
        in_specs=[
            SMEM,
            image_spec,
            pl.BlockSpec((group, tokens, width), block),
            pl.BlockSpec((2 * group, PAIR, width), block),
            pl.BlockSpec((2 * group, PAIR, width), block),
            pl.BlockSpec((group, tokens, 3 * width), block),
            pl.BlockSpec((2 * group, groups, stack, KEYS), block4),
            ANY,
            ANY,
            whole(choice.shape),
        ]
        + ([ANY] + [whole(s) for s in sums] if carried else []),
        out_specs=[image_spec] + [whole(s) for s, _ in outs],
        out_shape=[jax.ShapeDtypeStruct(images.shape, BF16)]
        + [jax.ShapeDtypeStruct(s, k) for s, k in outs],
        scratch_shapes=([pltpu.VMEM(s, F32) for s in sums] if last else [])
        + [
            pltpu.VMEM((group * tokens + COLS, 3 * width), BF16),
            pltpu.VMEM((group * tokens, 3 * width), BF16),
            *full,
            sems,
        ],
        input_output_aliases={10: 0} if carried else {},
        compiler_params=params(62),
        cost_estimate=pl.CostEstimate(
            flops=steps * group * tokens * width * width * 90,
            bytes_accessed=steps * group * 4 * MIB,
            transcendentals=0,
        ),
        name="attention_backward",
    )(ids, images, gres, gmix, mixed, triple, probs, *pieces, choice, *carried)


def expand_bias(table, seen, heads, per):
    return pl.pallas_call(
        bias_kernel,
        out_shape=jax.ShapeDtypeStruct((heads // per, per * PAIR, KEYS), F32),
        name="expand_bias",
    )(table, seen)


def flip(values, bits, devices):
    return lax.ppermute(values, "dev", [(i, i ^ bits) for i in range(devices)])


def exchange_groups(devices):
    bits = [1 << i for i in range(devices.bit_length() - 1)]
    return [bits[:1]] + [bits[i : i + 2] for i in range(1, len(bits), 2)]


def mixes(group):
    found = [0]
    for bit in group:
        found = found + [f ^ bit for f in found]
    return found


def block_order(devices):
    order = [0]
    for group in exchange_groups(devices)[:0:-1]:
        order = [m ^ o for m in mixes(group) for o in order]
    return order + [exchange_groups(devices)[0][0] ^ o for o in order]


def gather_parts(held, group, devices):
    return [held] + [flip(held, m, devices) for m in mixes(group)[1:]]


def gather_group(held, group, devices):
    return jnp.concatenate(gather_parts(held, group, devices))


def share_parts(held, group, devices):
    parts = jnp.split(held, 2 ** len(group))
    return parts[:1] + [flip(part, m, devices) for part, m in zip(parts[1:], mixes(group)[1:])]


def add_parts(parts):
    sums = [part.astype(F32) for part in parts]
    while len(sums) > 1:
        sums = [a + b for a, b in zip(sums[::2], sums[1::2])]
    return sums[0]


def tie(first, second):
    return lax.optimization_barrier((first, second))


def offsets():
    picks = np.full((2 * KEYS,), -1, np.int64)
    area = WINDOW * WINDOW
    for i in range(area):
        for j in range(area):
            place = (j // WINDOW - i // WINDOW) * COLS + j % WINDOW - i % WINDOW
            picks[place % (2 * KEYS)] = i * area + j
    return picks


def seen_keys():
    place = np.arange(KEYS)
    row, col = place // COLS, place % COLS
    side = np.where(col < SIDE, col // WINDOW, 2)
    ok = (row < WINDOW) & (side < 2)
    seen = (side[:PAIR, None] == side[None]) & ok[:PAIR, None] & ok[None]
    return seen.astype(np.float32)


def owner_lanes(vectors, me, devices):
    share = vectors.shape[-1]
    lane = lax.broadcasted_iota(jnp.int32, (1, share * devices), 1)
    return jnp.where(lane // share == me, jnp.tile(vectors, (1, devices)), 0)


def regroup(pieces, order, fields, me, devices, owners):
    by_number = np.argsort(np.array(order))
    blocks = jnp.concatenate(pieces)
    blocks = jnp.take(blocks, jnp.asarray(by_number)[jnp.arange(devices) ^ me], axis=0)
    out, at = [], 0
    for rows in fields:
        out.append(blocks[:, at : at + rows].reshape(owners, -1, blocks.shape[-1]))
        at += rows
    vectors = blocks[:, at:].reshape(owners, devices // owners, VEC_ROWS, -1)
    out.append(jnp.sum(vectors.astype(F32), 1).astype(BF16))
    return jnp.split(jnp.concatenate(out, 1), 2)


def ungroup(pieces, order, fields, me, devices, owners):
    blocks = jnp.concatenate(pieces)
    many = devices // owners
    out, at = [], 0
    for rows in fields:
        rows = rows * many
        out.append(blocks[:, at : at + rows].reshape(devices, rows // many, -1))
        at += rows
    out.append(jnp.repeat(blocks[:, at:], many, axis=0))
    blocks = jnp.take(jnp.concatenate(out, 1), jnp.asarray(np.array(order)) ^ me, axis=0)
    return jnp.split(blocks, 2)


def shards(
    devices,
    images,
    cotangent,
    image_counts,
    rel_index,
    ln1_gain,
    ln1_shift,
    w_qkv,
    q_bias,
    v_bias,
    w_proj,
    b_proj,
    ln2_gain,
    ln2_shift,
    w_fc1,
    b_fc1,
    w_fc2,
    b_fc2,
    bias_table,
):
    me = lax.axis_index("dev")
    slots, width = images.shape[0], images.shape[3]
    table_rows, heads = bias_table.shape
    own = ln1_gain.shape[0]
    span = b_fc1.shape[0]
    chunks = span // own
    per = LANES // (width // heads)
    groups = exchange_groups(devices)
    order = block_order(devices)
    aligned = own % COLS == 0
    owners = devices if aligned else width // COLS
    attn_fields = [own] * 3
    mlp_fields = [span] + [own] * (chunks + 1)
    if aligned:
        ids = jnp.asarray(np.array(order, np.int32)) ^ me
    else:
        ids = jnp.arange(owners, dtype=jnp.int32)

    attn_vec = owner_lanes(jnp.stack([ln1_gain, ln1_shift, q_bias, v_bias]), me, devices)
    attn_block = jnp.concatenate(
        [w_qkv[:, c * width : (c + 1) * width] for c in range(3)]
        + [attn_vec, jnp.zeros((VEC_ROWS - 4, width), BF16)]
    )
    mlp_vec = owner_lanes(jnp.stack([b_proj, ln2_gain, ln2_shift, b_fc2]), me, devices)
    hidden_vec = owner_lanes(b_fc1[None], me, devices).reshape(chunks, width)
    mlp_block = jnp.concatenate(
        [w_fc2]
        + [w_fc1[:, c * width : (c + 1) * width] for c in range(chunks)]
        + [w_proj, mlp_vec, hidden_vec, jnp.zeros((VEC_ROWS - 4 - chunks, width), BF16)]
    )
    far = groups[:0:-1]

    picks = offsets()
    rows_of = rel_index.reshape(-1)[np.maximum(picks, 0)]
    rows_of = jnp.where(jnp.asarray(picks) >= 0, rows_of, -1)
    choice = (rows_of[:, None] == jnp.arange(2 * KEYS, dtype=jnp.int32)).astype(BF16)
    table = jnp.pad(bias_table, ((0, 2 * KEYS - table_rows), (0, 0))).T
    high = table.astype(BF16)
    mid = (table - high.astype(F32)).astype(BF16)
    low = (table - high.astype(F32) - mid.astype(F32)).astype(BF16)
    by_offset = dot_nt(jnp.concatenate([high, mid, low]), choice)
    by_offset = by_offset[:heads] + by_offset[heads : 2 * heads] + by_offset[2 * heads :]
    bias = expand_bias(by_offset, jnp.asarray(seen_keys()), heads, per)

    attn_held, mlp_held = attn_block[None], mlp_block[None]
    for bits in far[:-1]:
        attn_held = gather_group(attn_held, bits, devices)
        attn_held, mlp_held = tie(attn_held, mlp_held)
        mlp_held = gather_group(mlp_held, bits, devices)
    attn_held = gather_group(attn_held, far[-1], devices)
    attn_held, mlp_held = tie(attn_held, mlp_held)
    bias, attn_held = tie(bias, attn_held)
    attn_pieces = (attn_held, flip(attn_held, groups[0][0], devices))
    if not aligned:
        attn_pieces = regroup(attn_pieces, order, attn_fields, me, devices, owners)

    group = image_group(slots)
    sizes = split_steps(slots // group, (5 / 6, 1 / 6))
    mlp_parts = gather_parts(mlp_held, far[-1], devices)
    carried, first = (), 0
    for steps in sizes:
        if carried:
            carried, mlp_parts = tie(carried, mlp_parts)
        carried = attention_forward(
            ids, images, attn_pieces, bias, heads, first, steps, group, carried
        )
        first += steps
    mlp_held = jnp.concatenate(mlp_parts)
    triple, raised, mixed, inverse = carried
    mlp_pieces = (mlp_held, flip(mlp_held, groups[0][0], devices))
    if not aligned:
        mlp_pieces = regroup(mlp_pieces, order, mlp_fields, me, devices, owners)
    output, gres, gmix, *mlp_sums = feed_forward(
        ids,
        image_counts,
        images,
        cotangent,
        mixed.reshape(slots, SIDE * COLS, width),
        inverse.reshape(slots, SIDE * COLS, width),
        mlp_pieces,
        chunks,
    )

    if not aligned:
        mlp_sums = ungroup(mlp_sums, order, mlp_fields, me, devices, owners)
    gmix = gmix.reshape(2 * slots, PAIR, width)
    sizes = split_steps(slots // group, (1 / 6, 1 / 2, 1 / 3))
    left = groups[1:]
    parts = [mlp_sums[0], flip(mlp_sums[1], groups[0][0], devices)]
    carried, first = (), 0
    for call, steps in enumerate(sizes):
        if carried:
            carried, parts = tie(carried, parts)
            if left:
                parts = share_parts(add_parts(parts).astype(BF16), left[0], devices)
                left = left[1:]
        carried = attention_backward(
            ids, images, gres, gmix, mixed, triple, raised, attn_pieces, choice, heads, first,
            steps, group, tuple(carried), call == len(sizes) - 1,
        )
        first += steps
    for bits in left:
        parts = share_parts(add_parts(parts).astype(BF16), bits, devices)
    if len(sizes) > 1:
        carried, parts = tie(carried, parts)
    mlp_mine = add_parts(parts).reshape(-1, width)

    grad_input, *attn_sums = carried
    if not aligned:
        attn_sums = ungroup(attn_sums, order, attn_fields, me, devices, owners)
    mine = add_parts([attn_sums[0], flip(attn_sums[1], groups[0][0], devices)])
    for bits in groups[1:]:
        mine = add_parts(share_parts(mine.astype(BF16), bits, devices))
    mine = mine.reshape(-1, width)

    grad_fc2 = mlp_mine[:span]
    at = span
    grad_fc1 = jnp.concatenate(
        [mlp_mine[at + c * own : at + (c + 1) * own] for c in range(chunks)], 1
    )
    at += chunks * own
    grad_proj = mlp_mine[at : at + own]
    at += own
    vectors = lax.dynamic_slice_in_dim(mlp_mine[at : at + 4], me * own, own, 1)
    grad_proj_bias, grad_gain_two, grad_shift_two, grad_fc2_bias = vectors
    grad_fc1_bias = lax.dynamic_slice_in_dim(
        mlp_mine[at + 4 : at + 4 + chunks].reshape(-1), me * span, span, 0
    )

    grad_qkv = jnp.concatenate([mine[c * own : (c + 1) * own] for c in range(3)], 1)
    tile = mine[3 * own :]
    table_total = tile[:heads, :table_rows].T
    vectors = tile[:, 2 * KEYS : 2 * KEYS + LANES].reshape(4, width)
    vectors = lax.dynamic_slice_in_dim(vectors, me * own, own, 1)
    grad_gain_one, grad_shift_one, grad_query_bias, grad_value_bias = vectors
    return (
        output,
        grad_input,
        grad_gain_one,
        grad_shift_one,
        grad_qkv,
        grad_query_bias,
        grad_value_bias,
        grad_proj,
        grad_proj_bias,
        grad_gain_two,
        grad_shift_two,
        grad_fc1,
        grad_fc1_bias,
        grad_fc2,
        grad_fc2_bias,
        table_total,
    )


def solution(mesh):
    rows = P("dev", None)
    image = P("dev", None, None, None)
    flat = P("dev")
    in_specs = (
        image, image, flat, P(), flat, flat, rows, flat, flat, rows, flat,
        flat, flat, rows, flat, rows, flat, P(),
    )
    out_specs = (
        image, image, flat, flat, rows, flat, flat, rows, flat,
        flat, flat, rows, flat, rows, flat, P(),
    )
    body = partial(shards, mesh.shape["dev"])
    return jax.shard_map(body, mesh=mesh, in_specs=in_specs, out_specs=out_specs, check_vma=False)
```
